128 devices in a mesh: bx: 8 (over y, core), by: 16 (over z, x).
Axes of the slice: x: 4, y: 4, z: 4, core: 2. Of those that a mesh axis runs over, the one named last changes fastest.
Arguments:
- features: bfloat16 [64, 128, 256, 128], P(None, 'bx', 'by'), may hold values from -6 to 6
- labels: int32 [128, 256, 128], P('bx', 'by'), may hold values from 0 to 255, as said below
- conv_weight: bfloat16 [64, 1728], replicated, may hold values from -0.15625 to 0.15625
- conv_bias: float32 [64], replicated, may hold values from -3 to 3
- head_weight: bfloat16 [3, 64], replicated, may hold values from -0.75 to 0.75
- head_bias: float32 [3], replicated, may hold values from -3 to 3
- edge_ends: int32 [128, 2, 512], P(('bx', 'by')), may hold values from 0 to 255
- edge_owner: int32 [128, 512, 1], P(('bx', 'by')), may hold values from 0 to 127; in each aligned block of 512 rows (0 to 511, 512 to 1023, ..., all dimensions but the last counted through in order) at most 8 rows name the same one
- edge_row: int32 [128, 512], P(('bx', 'by')), may hold values from 0 to 127
- edge_count: int32 [128], P(('bx', 'by')), may hold values from 128 to 512, as said below
Outputs:
- edge_weight: float32 [16384], P(('bx', 'by'))
The draws below stay inside these ranges and needn't reach their ends.
Inputs may be any that keep to these rules, and one draw needn't show every extreme that they name: `labels`: supervoxels are spatially coherent regions. `edge_owner`: no owner is named by more than 8 of one brick's 512 slots, a bound that some block reaches. `edge_count`: some brick has all 512 slots live.
All inputs are finite; a program needn't handle non-finite values.
Results may differ from the reference program's by a relative error of at most 0.0003.
Values may be sent and summed in bfloat16 or wider, within the bound.
A program may use at most 128 MiB of HBM per device.

```python
import math
import jax
import jax.numpy as jnp
import numpy as np
from jax import lax

C = 64
CX = 16
CY = 16
CZ = 128
LABELS = 256
EB = 512
EO = 128
CAP = 8
NX = 128
NY = 256
N_BX = 8
N_BY = 16


def region_layout(key):
    side_x = max(2, CX // 2)
    side_y = max(2, CY // 2)
    side_z = max(2, CZ // 8)
    grid_x = NX // side_x + 2
    grid_y = NY // side_y + 2
    grid_z = CZ // side_z + 2
    subkeys = jax.random.split(key, 4)
    shift_x = jax.random.randint(subkeys[0], (grid_y, grid_z), 0, side_x, dtype=jnp.int32)
    shift_y = jax.random.randint(subkeys[1], (grid_x, grid_z), 0, side_y, dtype=jnp.int32)
    shift_z = jax.random.randint(subkeys[2], (grid_x, grid_y), 0, side_z, dtype=jnp.int32)
    id_table = jax.random.randint(subkeys[3], (grid_x, grid_y, grid_z), 0, LABELS, dtype=jnp.int32)
    return ((side_x, side_y, side_z), (shift_x, shift_y, shift_z), id_table)


def box_indices(coord_x, coord_y, coord_z, layout):
    sides, shifts, id_table = layout
    box_x = (coord_x + shifts[0][coord_y // sides[1], coord_z // sides[2]]) // sides[0]
    box_y = (coord_y + shifts[1][coord_x // sides[0], coord_z // sides[2]]) // sides[1]
    box_z = (coord_z + shifts[2][coord_x // sides[0], coord_y // sides[1]]) // sides[2]
    return (box_x, box_y, box_z)


def label_at(coord_x, coord_y, coord_z, layout):
    coord_x = jnp.clip(coord_x, 0, NX - 1)
    coord_y = jnp.clip(coord_y, 0, NY - 1)
    coord_z = jnp.clip(coord_z, 0, CZ - 1)
    box_x, box_y, box_z = box_indices(coord_x, coord_y, coord_z, layout)
    return layout[2][box_x, box_y, box_z]


def draw_labels(key, part):
    layout = region_layout(key)
    coord_x = jnp.broadcast_to(jnp.arange(NX, dtype=jnp.int32)[:, None, None], (NX, NY, CZ))
    coord_y = jnp.broadcast_to(jnp.arange(NY, dtype=jnp.int32)[None, :, None], (NX, NY, CZ))
    coord_z = jnp.broadcast_to(jnp.arange(CZ, dtype=jnp.int32)[None, None, :], (NX, NY, CZ))
    return label_at(coord_x, coord_y, coord_z, layout).astype(jnp.int32)


def draw_edge_ends(key, part):
    layout = region_layout(key)
    key = jax.random.fold_in(key, 7)
    subkeys = jax.random.split(key, 4)
    bricks = N_BX * N_BY
    brick = jnp.arange(bricks, dtype=jnp.int32)[:, None]
    coord_x = brick // N_BY * CX + jax.random.randint(subkeys[0], (bricks, EB), 0, CX, dtype=jnp.int32)
    coord_y = brick % N_BY * CY + jax.random.randint(subkeys[1], (bricks, EB), 0, CY, dtype=jnp.int32)
    coord_z = jax.random.randint(subkeys[2], (bricks, EB), 0, CZ, dtype=jnp.int32)
    heading = jax.random.randint(subkeys[3], (bricks, EB), 0, 3, dtype=jnp.int32)
    sides, shifts, id_table = layout
    box_x, box_y, box_z = box_indices(coord_x, coord_y, coord_z, layout)
    start_x = box_x * sides[0] - shifts[0][coord_y // sides[1], coord_z // sides[2]]
    start_y = box_y * sides[1] - shifts[1][coord_x // sides[0], coord_z // sides[2]]
    start_z = box_z * sides[2] - shifts[2][coord_x // sides[0], coord_y // sides[1]]
    upper_x = jnp.where(heading == 0, start_x, coord_x)
    upper_y = jnp.where(heading == 1, start_y, coord_y)
    upper_z = jnp.where(heading == 2, start_z, coord_z)
    lower_x = upper_x - (heading == 0).astype(jnp.int32)
    lower_y = upper_y - (heading == 1).astype(jnp.int32)
    lower_z = upper_z - (heading == 2).astype(jnp.int32)
    first = label_at(upper_x, upper_y, upper_z, layout)
    second = label_at(lower_x, lower_y, lower_z, layout)
    return jnp.stack([first, second], axis=1).astype(jnp.int32)


def draw_edge_count(key, part):
    key = jax.random.fold_in(key, 11)
    first, second = jax.random.split(key)
    devices = N_BX * N_BY
    counts = jax.random.randint(first, (devices,), EB // 4, EB + 1, dtype=jnp.int32)
    full_at = jax.random.randint(second, (), 0, devices, dtype=jnp.int32)
    return jnp.where(jnp.arange(devices, dtype=jnp.int32) == full_at, jnp.int32(EB), counts)


def set_ends(drawn, rng, least, largest):
    longest = drawn.shape.index(max(drawn.shape))
    spots = []
    for shift in (0, 1):
        where = [jax.random.randint(jax.random.fold_in(rng, axis), (), 0, length) for axis, length in enumerate(drawn.shape)]
        where[longest] = (where[longest] + shift) % drawn.shape[longest]
        spots.append(tuple(where))
    return drawn.at[spots[0]].set(least).at[spots[1]].set(largest)


def level_of(rng, dims, cuts, least, high):
    def one(dim, shards_of):
        heights = jax.random.uniform(jax.random.fold_in(jax.random.fold_in(rng, 6), dim), (shards_of,), jnp.float32, least / len(cuts), high / len(cuts))
        return jnp.repeat(jnp.exp(heights), dims[dim] // shards_of).reshape((-1,) + (1,) * (len(dims) - dim - 1))

    level = one(*cuts[0])
    for cut in cuts[1:]:
        level = level * one(*cut)
    return level


def assign_block(own_key, own, number, rows, amount, top, limit, slope):
    order = jax.random.permutation(own_key, amount)
    packed, common = shares(amount, rows * top, limit, slope, True), shares(amount, rows * top, limit, slope, False)
    places = jnp.arange(amount)

    def named(tallies, offset_by):
        used = int((tallies > 0).sum())
        fixed = max(1, used // 4)
        passed = fixed + (places - fixed + offset_by * (used - fixed)) % max(1, amount - fixed)
        return jnp.zeros((amount,), jnp.int32).at[order[jnp.where(places < fixed, places, passed)]].set(jnp.asarray(tallies, jnp.int32))

    tallies = jnp.where(number % 4 == 0, named(packed, number // 4), named(common, number - number // 4 - 1))
    mixed = jax.random.permutation(jax.random.fold_in(own, 3), amount)
    donor, receiver = mixed[0:amount // 2 * 2:2], mixed[1:amount // 2 * 2:2]
    room = jnp.minimum(tallies[donor] - 1, limit - tallies[receiver]) // 2
    room = jnp.where((donor == order[0]) | (receiver == order[0]) | (tallies[receiver] == 0), 0, jnp.maximum(room, 0))
    passed = jax.random.randint(jax.random.fold_in(own, 4), (amount // 2,), 0, 1 << 20) % (room + 1)
    tallies = tallies.at[donor].add(-passed).at[receiver].add(passed)
    members = jnp.searchsorted(jnp.cumsum(tallies), jnp.arange(rows * top), side="right").astype(jnp.int32)
    listing = members.reshape(top, rows).T
    listing = listing[jax.random.permutation(jax.random.fold_in(own, 1), rows)]
    offset_by = jax.random.randint(jax.random.fold_in(own, 2), (rows, 1), 0, top)
    return jnp.take_along_axis(listing, (jnp.arange(top)[None, :] + offset_by) % top, axis=1)


def shares(count, total, bound, slope, full):
    loads = [(1 << 20) // math.isqrt(standing ** slope) + 1 for standing in range(1, count + 1)]
    largest = bound if full else min(bound, max(-(-total // count), total * loads[0] // sum(loads)))
    least = 1 if total - largest >= count - 1 else 0
    holding, rest = [largest] + [least] * (count - 1), total - largest - least * (count - 1)
    while rest > 0:
        candidates = [i for i in range(1, count) if holding[i] < largest] or [i for i in range(1, count) if holding[i] < bound]
        mass, remaining = sum([loads[i] for i in candidates]), rest
        for i in candidates:
            more = min(bound - holding[i], max(1, remaining * loads[i] // mass), rest)
            holding[i] = holding[i] + more
            rest = rest - more
    return np.array(holding)


def bell_draw(rng, extent, spread, most, cuts=(), kind=jnp.bfloat16):
    values = jax.random.normal(rng, extent, jnp.float32) * spread
    if len(cuts) > 0:
        values = level_of(rng, extent, cuts, -0.22, 0.18) * values
    return jnp.clip(values, min=-most, max=most).astype(kind)


def setup_inputs(seed: int = 0) -> dict:
    key_of = jax.random.split(jax.random.key(seed), 11)
    features = bell_draw(key_of[0], (C, NX, NY, CZ), 1.0, 6.0, ((1, 8), (2, 16)))
    labels = draw_labels(jax.random.fold_in(key_of[10], 71), 0)
    conv_weight = bell_draw(key_of[2], (C, 27 * C), (27 * C) ** -0.5, 0.15625)
    conv_bias = bell_draw(key_of[3], (C,), 0.5, 3.0, (), jnp.float32)
    head_weight = bell_draw(key_of[4], (3, C), C ** -0.5, 0.75)
    head_bias = bell_draw(key_of[5], (3,), 1.0, 3.0, (), jnp.float32)
    edge_ends = draw_edge_ends(jax.random.fold_in(key_of[10], 71), 0)
    edge_owner_keys = jax.random.split(jax.random.fold_in(key_of[7], 1), (N_BX * N_BY) * EB // EB)
    edge_owner_turns = jax.random.permutation(jax.random.fold_in(key_of[7], 3), (N_BX * N_BY) * EB // EB)
    edge_owner = jax.vmap(lambda own, number: assign_block(jax.random.fold_in(key_of[7], 2), own, number, EB, N_BX * N_BY, 1, CAP, 2))(edge_owner_keys, edge_owner_turns).reshape((N_BX * N_BY, EB, 1))
    edge_row = set_ends(jax.random.randint(key_of[8], (N_BX * N_BY, EB), 0, EO), jax.random.fold_in(key_of[8], 1), 0, EO - 1).astype(jnp.int32)
    edge_count = draw_edge_count(jax.random.fold_in(key_of[10], 71), 0)
    return {"features": features, "labels": labels, "conv_weight": conv_weight, "conv_bias": conv_bias, "head_weight": head_weight, "head_bias": head_bias, "edge_ends": edge_ends, "edge_owner": edge_owner, "edge_row": edge_row, "edge_count": edge_count}


def brick_sums(padded, labels, below_x, below_y, below_z, conv_weight, conv_bias, head_weight, head_bias, ends, live):
    chans = padded.shape[0]
    planes = labels.shape[0]
    rows = labels.shape[1]
    depth = labels.shape[2]
    weight_full = conv_weight.astype(jnp.float32)
    head_full = head_weight.astype(jnp.float32)
    label_ids = jnp.arange(LABELS, dtype=jnp.int32)

    def one_block(start):
        block = lax.dynamic_slice_in_dim(padded, start, 4, 1)
        taps = jnp.stack([block[:, dx:dx + 2, dy:dy + rows, dz:dz + depth]
                          for dx in range(3) for dy in range(3) for dz in range(3)], 0)
        taps = taps.reshape(27 * chans, 2 * rows * depth).astype(jnp.float32)
        pre = jnp.dot(weight_full, taps, precision=lax.Precision.HIGHEST) + conv_bias[:, None]
        hidden = jnp.maximum(pre, 0.0).astype(jnp.bfloat16)
        logits = jnp.dot(head_full, hidden.astype(jnp.float32), precision=lax.Precision.HIGHEST) + head_bias[:, None]
        rounded = lax.optimization_barrier(jax.nn.sigmoid(logits).astype(jnp.bfloat16))
        affin = rounded.astype(jnp.float32).reshape(-1)
        own = lax.dynamic_slice_in_dim(labels, start, 2, 0).reshape(-1)
        others = jnp.concatenate([lax.dynamic_slice_in_dim(neighbour, start, 2, 0).reshape(-1)
                                  for neighbour in (below_x, below_y, below_z)], 0)
        owns = jnp.concatenate([own, own, own], 0)
        left = (owns[:, None] == label_ids[None, :]).astype(jnp.float32)
        right = jnp.where(others[:, None] == label_ids[None, :], affin[:, None], jnp.float32(0.0))
        return jnp.dot(left.T, right, precision=lax.Precision.HIGHEST)

    starts = jnp.arange(0, planes, 2, dtype=jnp.int32)
    pair_table = jnp.sum(lax.map(one_block, starts), axis=0)
    keep = 1.0 - jnp.eye(LABELS, dtype=jnp.float32)
    symmetric = ((pair_table + pair_table.T) * keep).reshape(-1)
    return symmetric[ends[0] * LABELS + ends[1]] * live


def reference(features, labels, conv_weight, conv_bias, head_weight, head_bias, edge_ends, edge_owner, edge_row, edge_count):
    padded = jnp.pad(features, ((0, 0), (1, 1), (1, 1), (1, 1)))
    lowered = jnp.pad(labels, ((1, 0), (1, 0), (1, 0)), constant_values=-1)
    below_x = lowered[:-1, 1:, 1:]
    below_y = lowered[1:, :-1, 1:]
    below_z = lowered[1:, 1:, :-1]
    zero = jnp.int32(0)

    def brick(index):
        x_start = (index // N_BY) * CX
        y_start = (index % N_BY) * CY
        pad_brick = lax.dynamic_slice(padded, (zero, x_start, y_start, zero), (C, CX + 2, CY + 2, CZ + 2))

        def cut(field):
            return lax.dynamic_slice(field, (x_start, y_start, zero), (CX, CY, CZ))

        live = (jnp.arange(EB, dtype=jnp.int32) < edge_count[index]).astype(jnp.float32)
        return brick_sums(pad_brick, cut(labels), cut(below_x), cut(below_y), cut(below_z),
                          conv_weight, conv_bias, head_weight, head_bias, edge_ends[index], live)

    partials = lax.map(brick, jnp.arange(N_BX * N_BY, dtype=jnp.int32))
    target = (edge_owner[:, :, 0] * EO + edge_row).reshape(-1)
    return jnp.zeros((EO * N_BX * N_BY,), jnp.float32).at[target].add(partials.reshape(-1))
```

```python
import functools

import jax
import jax.numpy as jnp
from jax import lax
from jax.experimental import pallas as pl
from jax.experimental.pallas import tpu as pltpu
from jax.sharding import PartitionSpec as P

LABELS = 256
EO = 128
NBX = 8
NBY = 16
CX = 16
CY = 16
CZ = 128
C = 64
SLOTS = 512
MESH = pl.DeviceIdType.MESH
VMEM = pl.BlockSpec(memory_space=pltpu.VMEM)


def halo_kernel(f_ref, lab_ref, perm_ref, p_ref, lx_ref, ly_ref, rows_ref, send_sem, recv_sem):
    bx = lax.axis_index("bx")
    by = lax.axis_index("by")
    xm = lax.rem(bx + NBX - 1, NBX)
    xp = lax.rem(bx + 1, NBX)
    ym = lax.rem(by + NBY - 1, NBY)
    yp = lax.rem(by + 1, NBY)
    around = [(xm, by), (xp, by), (bx, ym), (bx, yp), (xm, ym), (xm, yp), (xp, ym), (xp, yp)]
    barrier = pltpu.get_barrier_semaphore()
    for peer in around:
        pl.semaphore_signal(barrier, inc=1, device_id=peer, device_id_type=MESH)

    rows_ref[...] = lab_ref[:, CY - 1, :]
    perm = perm_ref[...]

    def turned(pair, carry):
        for group in range(C // 16):
            block = jnp.concatenate(
                [
                    f_ref[16 * group : 16 * group + 16, 2 * pair + half].reshape(256, CZ)
                    for half in range(2)
                ],
                axis=1,
            )
            out = jnp.dot(perm, block, preferred_element_type=jnp.float32).astype(jnp.bfloat16)
            for half in range(2):
                p_ref[1 + 2 * pair + half, 1 : CY + 1, 16 * group : 16 * group + 16, :] = out[
                    :, half * CZ : (half + 1) * CZ
                ].reshape(CY, 16, CZ)
        return carry

    lax.fori_loop(0, CX // 2, turned, 0)
    pl.semaphore_wait(barrier, len(around))
    inner = pl.ds(1, CX)
    copies = []

    def send(src, dst, peer):
        at = len(copies)
        copy = pltpu.make_async_remote_copy(
            src_ref=src,
            dst_ref=dst,
            send_sem=send_sem.at[at],
            recv_sem=recv_sem.at[at],
            device_id=peer,
            device_id_type=MESH,
        )
        copy.start()
        copies.append(copy)

    send(p_ref.at[1, inner], p_ref.at[CX + 1, inner], (xm, by))
    send(p_ref.at[CX, inner], p_ref.at[0, inner], (xp, by))
    send(p_ref.at[inner, 1], p_ref.at[inner, CY + 1], (bx, ym))
    send(p_ref.at[inner, CY], p_ref.at[inner, 0], (bx, yp))
    send(p_ref.at[1, 1], p_ref.at[CX + 1, CY + 1], (xm, ym))
    send(p_ref.at[1, CY], p_ref.at[CX + 1, 0], (xm, yp))
    send(p_ref.at[CX, 1], p_ref.at[0, CY + 1], (xp, ym))
    send(p_ref.at[CX, CY], p_ref.at[0, 0], (xp, yp))
    send(lab_ref.at[CX - 1], lx_ref, (xp, by))
    send(rows_ref, ly_ref, (bx, yp))
    for copy in copies:
        copy.wait()

    @pl.when(bx == 0)
    def _():
        p_ref[0] = jnp.zeros((CY + 2, C, CZ), jnp.bfloat16)
        lx_ref[...] = jnp.full((CY, CZ), -1, jnp.int32)

    @pl.when(bx == NBX - 1)
    def _():
        p_ref[CX + 1] = jnp.zeros((CY + 2, C, CZ), jnp.bfloat16)

    @pl.when(by == 0)
    def _():
        p_ref[:, 0] = jnp.zeros((CX + 2, C, CZ), jnp.bfloat16)
        ly_ref[...] = jnp.full((CX, CZ), -1, jnp.int32)

    @pl.when(by == NBY - 1)
    def _():
        p_ref[:, CY + 1] = jnp.zeros((CX + 2, C, CZ), jnp.bfloat16)


def brick_kernel(
    p0_ref,
    p1_ref,
    p2_ref,
    own_ref,
    ox_ref,
    ly_ref,
    w_ref,
    bias_ref,
    head_ref,
    head_bias_ref,
    ends_ref,
    owner_ref,
    row_ref,
    count_ref,
    out_ref,
    logit_ref,
    table_ref,
):
    x = pl.program_id(0)
    lane = lax.broadcasted_iota(jnp.int32, (2 * C, CZ), 1)
    weights = w_ref[...]
    planes = [ref[0].reshape((CY + 2) * C, CZ) for ref in (p0_ref, p1_ref, p2_ref)]
    for t in range(4):
        low = 2 * t * C
        high = low + 8 * C
        stacked = jnp.concatenate(
            [
                jnp.concatenate([plane[low : low + 4 * C], plane[high : high + 4 * C]], axis=1)
                for plane in planes
            ],
            axis=0,
        )
        sums = jnp.dot(weights, stacked, preferred_element_type=jnp.float32)
        halves = []
        for half in range(2):
            part = sums[:, half * CZ : (half + 1) * CZ]
            before = pltpu.roll(part[: 2 * C], 1, 1)
            after = pltpu.roll(part[4 * C :], CZ - 1, 1)
            pre = (
                part[2 * C : 4 * C]
                + jnp.where(lane > 0, before, 0.0)
                + jnp.where(lane < CZ - 1, after, 0.0)
                + bias_ref[...]
            )
            halves.append(jnp.maximum(pre, 0.0).astype(jnp.bfloat16))
        hidden = jnp.concatenate(halves, axis=1)
        logits = jnp.dot(head_ref[...], hidden, preferred_element_type=jnp.float32)
        for d in range(3):
            for half in range(2):
                logit_ref[d, 2 * t + 8 * half : 2 * t + 8 * half + 2, :] = logits[
                    2 * d : 2 * d + 2, half * CZ : (half + 1) * CZ
                ]

    affin = [
        jax.nn.sigmoid(logit_ref[d] + head_bias_ref[d]).astype(jnp.bfloat16).astype(jnp.float32)
        for d in range(3)
    ]
    own_i = own_ref[0]
    line = lax.broadcasted_iota(jnp.int32, (CY, CZ), 0)
    deep = lax.broadcasted_iota(jnp.int32, (CY, CZ), 1)
    edge_line = jnp.broadcast_to(ly_ref[pl.ds(x, 1), :], (CY, CZ))
    own = own_i.astype(jnp.float32)
    oth_x = ox_ref[0].astype(jnp.float32)
    oth_y = jnp.where(line > 0, pltpu.roll(own_i, 1, 0), edge_line).astype(jnp.float32)
    oth_z = jnp.where(deep > 0, pltpu.roll(own_i, 1, 1), -1).astype(jnp.float32)
    same_xy = oth_x == oth_y
    same_xz = oth_x == oth_z
    same_yz = oth_y == oth_z
    sum_x = affin[0] + jnp.where(same_xy, affin[1], 0.0) + jnp.where(same_xz, affin[2], 0.0)
    sum_y = affin[1] + jnp.where(same_yz, affin[2], 0.0)
    top_x = sum_x.astype(jnp.bfloat16).astype(jnp.float32)
    top_y = sum_y.astype(jnp.bfloat16).astype(jnp.float32)
    in_x = same_xy | same_xz
    rest = jnp.where(in_x, sum_x - top_x, sum_y - top_y)
    rest_at = jnp.where(in_x, oth_x, oth_y)

    ids = lax.broadcasted_iota(jnp.int32, (LABELS, CZ), 0).astype(jnp.float32).astype(jnp.bfloat16)

    def spread_row(values, y):
        wide = jnp.broadcast_to(values[y : y + 1, :], (16, CZ)).astype(jnp.bfloat16)
        return jnp.concatenate([wide] * (LABELS // 16), axis=0)

    zero = jnp.zeros((LABELS, CZ), jnp.bfloat16)
    one = jnp.ones((LABELS, CZ), jnp.bfloat16)
    lefts, tops, rests = [], [], []
    for y in range(CY):
        lefts.append(jnp.where(spread_row(own, y) == ids, one, zero))
        tops.append(
            jnp.where(
                spread_row(oth_x, y) == ids,
                spread_row(top_x, y),
                jnp.where(
                    spread_row(oth_y, y) == ids,
                    spread_row(top_y, y),
                    jnp.where(spread_row(oth_z, y) == ids, spread_row(affin[2], y), zero),
                ),
            )
        )
        rests.append(jnp.where(spread_row(rest_at, y) == ids, spread_row(rest, y), zero))
    left = jnp.concatenate(lefts, axis=1)
    right = jnp.concatenate(
        [jnp.concatenate(tops, axis=1), jnp.concatenate(rests, axis=1)], axis=0
    )
    found = lax.dot_general(
        right, left, (((1,), (1,)), ((), ())), preferred_element_type=jnp.float32
    )
    found = found[:LABELS] + found[LABELS:]

    @pl.when(x == 0)
    def _():
        table_ref[...] = found

    @pl.when(x > 0)
    def _():
        table_ref[...] += found

    @pl.when(x == CX - 1)
    def _():
        table = table_ref[...]
        first = ends_ref[0:1, :]
        second = ends_ref[1:2, :]
        label = lax.broadcasted_iota(jnp.int32, (LABELS, SLOTS), 0)
        slot = lax.broadcasted_iota(jnp.int32, (1, SLOTS), 1)
        picked = jnp.dot(
            table + table.T,
            (first == label).astype(jnp.float32),
            precision=lax.Precision.HIGHEST,
            preferred_element_type=jnp.float32,
        )
        value = jnp.sum(jnp.where(second == label, picked, 0.0), axis=0, keepdims=True)
        keep = (slot < count_ref[0]) & (first != second)
        value = jnp.where(keep, value, 0.0)
        owner = owner_ref[...]
        place = (owner % NBY) * NBX + owner // NBY
        row_id = lax.broadcasted_iota(jnp.int32, (EO, SLOTS), 0)
        out_ref[...] = lax.dot_general(
            jnp.where(place == row_id, value, 0.0),
            (row_ref[...] == row_id).astype(jnp.float32),
            (((1,), (1,)), ((), ())),
            precision=lax.Precision.HIGHEST,
            preferred_element_type=jnp.float32,
        )


def gather_kernel(s_ref, o_ref, got_ref, mid_ref, last_ref, send1, recv1, send2, recv2):
    bx = lax.axis_index("bx")
    by = lax.axis_index("by")
    barrier = pltpu.get_barrier_semaphore()
    for step in range(1, NBY):
        peer = (bx, lax.rem(by + step, NBY))
        pl.semaphore_signal(barrier, inc=1, device_id=peer, device_id_type=MESH)
    for step in range(1, NBX):
        peer = (lax.rem(bx + step, NBX), by)
        pl.semaphore_signal(barrier, inc=1, device_id=peer, device_id_type=MESH)
    pl.semaphore_wait(barrier, NBX + NBY - 2)
    copies = []
    for step in range(1, NBY):
        to = lax.rem(by + step, NBY)
        copy = pltpu.make_async_remote_copy(
            src_ref=s_ref.at[to],
            dst_ref=got_ref.at[step],
            send_sem=send1.at[step],
            recv_sem=recv1.at[step],
            device_id=(bx, to),
            device_id_type=MESH,
        )
        copy.start()
        copies.append(copy)
    total = s_ref[by]
    for step in range(1, NBY):
        copies[step - 1].wait()
        total = total + got_ref[step]
    for row in range(NBX):
        mid_ref[row] = total[row : row + 1, :]
    copies = []
    for step in range(1, NBX):
        to = lax.rem(bx + step, NBX)
        copy = pltpu.make_async_remote_copy(
            src_ref=mid_ref.at[to],
            dst_ref=last_ref.at[step],
            send_sem=send2.at[step],
            recv_sem=recv2.at[step],
            device_id=(to, by),
            device_id_type=MESH,
        )
        copy.start()
        copies.append(copy)
    total = mid_ref[bx]
    for step in range(1, NBX):
        copies[step - 1].wait()
        total = total + last_ref[step]
    o_ref[...] = total


def on_device(
    features,
    labels,
    conv_weight,
    conv_bias,
    head_weight,
    head_bias,
    edge_ends,
    edge_owner,
    edge_row,
    edge_count,
):
    spot = jnp.arange(256, dtype=jnp.int32)
    perm = ((spot[:, None] % 16) * 16 + spot[:, None] // 16 == spot[None, :]).astype(jnp.bfloat16)
    padded, plane, edge_line = pl.pallas_call(
        halo_kernel,
        out_shape=(
            jax.ShapeDtypeStruct((CX + 2, CY + 2, C, CZ), jnp.bfloat16),
            jax.ShapeDtypeStruct((CY, CZ), jnp.int32),
            jax.ShapeDtypeStruct((CX, CZ), jnp.int32),
        ),
        in_specs=[VMEM] * 3,
        out_specs=(VMEM,) * 3,
        scratch_shapes=[
            pltpu.VMEM((CX, CZ), jnp.int32),
            pltpu.SemaphoreType.DMA((10,)),
            pltpu.SemaphoreType.DMA((10,)),
        ],
        compiler_params=pltpu.CompilerParams(
            collective_id=0, has_side_effects=True, vmem_limit_bytes=40 * 2**20
        ),
        name="halo",
    )(features, labels, perm)

    taps = conv_weight.reshape(C, 3, 3, 3, C).transpose(3, 0, 1, 2, 4)
    wide = jnp.stack(
        [
            jnp.pad(taps, ((0, 0), (0, 0), (0, 0), (0, 1), (0, 0))),
            jnp.pad(taps, ((0, 0), (0, 0), (0, 0), (1, 0), (0, 0))),
        ],
        axis=1,
    ).reshape(6 * C, 12 * C)
    bias = jnp.broadcast_to(jnp.concatenate([conv_bias, conv_bias])[:, None], (2 * C, CZ))
    blank = jnp.zeros((3, C), jnp.bfloat16)
    head = jnp.stack(
        [
            jnp.concatenate([head_weight, blank], axis=1),
            jnp.concatenate([blank, head_weight], axis=1),
        ],
        axis=1,
    ).reshape(6, 2 * C)
    head = jnp.pad(head, ((0, 10), (0, 0)))
    below_x = jnp.concatenate([plane[None], labels[:-1]], axis=0)

    def whole(*shape):
        return pl.BlockSpec(shape, lambda x: (0,) * len(shape))

    spread = pl.pallas_call(
        brick_kernel,
        grid=(CX,),
        out_shape=jax.ShapeDtypeStruct((EO, EO), jnp.float32),
        in_specs=[
            pl.BlockSpec((1, CY + 2, C, CZ), lambda x: (x, 0, 0, 0)),
            pl.BlockSpec((1, CY + 2, C, CZ), lambda x: (x + 1, 0, 0, 0)),
            pl.BlockSpec((1, CY + 2, C, CZ), lambda x: (x + 2, 0, 0, 0)),
            pl.BlockSpec((1, CY, CZ), lambda x: (x, 0, 0)),
            pl.BlockSpec((1, CY, CZ), lambda x: (x, 0, 0)),
            whole(CX, CZ),
            whole(6 * C, 12 * C),
            whole(2 * C, CZ),
            whole(16, 2 * C),
            pl.BlockSpec(memory_space=pltpu.SMEM),
            whole(2, SLOTS),
            whole(1, SLOTS),
            whole(1, SLOTS),
            pl.BlockSpec(memory_space=pltpu.SMEM),
        ],
        out_specs=whole(EO, EO),
        scratch_shapes=[
            pltpu.VMEM((3, CY, CZ), jnp.float32),
            pltpu.VMEM((LABELS, LABELS), jnp.float32),
        ],
        compiler_params=pltpu.CompilerParams(vmem_limit_bytes=48 * 2**20),
        name="brick",
    )(
        padded,
        padded,
        padded,
        labels,
        below_x,
        edge_line,
        wide,
        bias,
        head,
        head_bias,
        edge_ends[0],
        edge_owner[:, :, 0],
        edge_row,
        edge_count,
    )

    total = pl.pallas_call(
        gather_kernel,
        out_shape=jax.ShapeDtypeStruct((1, EO), jnp.float32),
        in_specs=[VMEM],
        out_specs=VMEM,
        scratch_shapes=[
            pltpu.VMEM((NBY, NBX, EO), jnp.float32),
            pltpu.VMEM((NBX, 1, EO), jnp.float32),
            pltpu.VMEM((NBX, 1, EO), jnp.float32),
            pltpu.SemaphoreType.DMA((NBY,)),
            pltpu.SemaphoreType.DMA((NBY,)),
            pltpu.SemaphoreType.DMA((NBX,)),
            pltpu.SemaphoreType.DMA((NBX,)),
        ],
        compiler_params=pltpu.CompilerParams(collective_id=1, has_side_effects=True),
        name="owners",
    )(spread.reshape(NBY, NBX, EO))
    return total[0]


def solution(mesh):
    placed = (
        P(None, "bx", "by", None),
        P("bx", "by", None),
        P(),
        P(),
        P(),
        P(),
        P(("bx", "by"), None, None),
        P(("bx", "by"), None, None),
        P(("bx", "by"), None),
        P(("bx", "by")),
    )
    return jax.shard_map(
        on_device, mesh=mesh, in_specs=placed, out_specs=P(("bx", "by")), check_vma=False
    )
```

```python
import jax
import jax.numpy as jnp
from jax import lax
from jax.experimental import pallas as pl
from jax.experimental.pallas import tpu as pltpu
from jax.sharding import PartitionSpec as P

LABELS = 256
EO = 128
NBX = 8
NBY = 16
CX = 16
CY = 16
CZ = 128
C = 64
SLOTS = 512
PAIRS = CY // 2
MESH = pl.DeviceIdType.MESH
VMEM = pl.BlockSpec(memory_space=pltpu.VMEM)
SMEM = pl.BlockSpec(memory_space=pltpu.SMEM)


def lay_weights(conv_ref, w_ref):
    blank = jnp.zeros((C, C), jnp.bfloat16)
    for dz in range(3):
        for out_y in range(2):
            pieces = []
            for dx in range(3):
                for in_y in range(4):
                    dy = in_y - out_y
                    at = (9 * dx + 3 * dy + dz) * C
                    pieces.append(conv_ref[:, at : at + C] if 0 <= dy <= 2 else blank)
            w_ref[(2 * dz + out_y) * C : (2 * dz + out_y + 1) * C, :] = jnp.concatenate(
                pieces, axis=1
            )


def conv_plane(x, p_ref, w_ref, bias_ref, head_ref, head_bias_ref, logit_ref):
    lane = lax.broadcasted_iota(jnp.int32, (2 * C, CZ), 1)
    stacked = jnp.concatenate(
        [
            jnp.concatenate(
                [p_ref[x + dx, 2 * j : 2 * j + 4].reshape(4 * C, CZ) for j in range(PAIRS)], axis=1
            )
            for dx in range(3)
        ],
        axis=0,
    )
    sums = jnp.dot(w_ref[...], stacked, preferred_element_type=jnp.float32)
    parts = []
    for j in range(PAIRS):
        part = sums[:, j * CZ : (j + 1) * CZ]
        before = pltpu.roll(part[: 2 * C], 1, 1)
        after = pltpu.roll(part[4 * C :], CZ - 1, 1)
        pre = (
            part[2 * C : 4 * C]
            + jnp.where(lane > 0, before, 0.0)
            + jnp.where(lane < CZ - 1, after, 0.0)
            + bias_ref[...]
        )
        parts.append(jnp.maximum(pre, 0.0).astype(jnp.bfloat16))
    hidden = jnp.concatenate(parts, axis=1)
    logits = jnp.dot(head_ref[...], hidden, preferred_element_type=jnp.float32)
    for d in range(3):
        for j in range(PAIRS):
            logit_ref[d, 2 * j : 2 * j + 2, :] = (
                logits[2 * d : 2 * d + 2, j * CZ : (j + 1) * CZ] + head_bias_ref[d]
            )


def pair_sums(x, logit_ref, lab_ref, line_ref):
    affin = [
        jax.nn.sigmoid(logit_ref[d]).astype(jnp.bfloat16).astype(jnp.float32) for d in range(3)
    ]
    own_i = lab_ref[x + 1]
    line = lax.broadcasted_iota(jnp.int32, (CY, CZ), 0)
    deep = lax.broadcasted_iota(jnp.int32, (CY, CZ), 1)
    edge_line = jnp.broadcast_to(line_ref[pl.ds(x, 1), :], (CY, CZ))
    own = own_i.astype(jnp.float32)
    oth_x = lab_ref[x].astype(jnp.float32)
    oth_y = jnp.where(line > 0, pltpu.roll(own_i, 1, 0), edge_line).astype(jnp.float32)
    oth_z = jnp.where(deep > 0, pltpu.roll(own_i, 1, 1), -1).astype(jnp.float32)
    same_xy = oth_x == oth_y
    same_xz = oth_x == oth_z
    same_yz = oth_y == oth_z
    sum_x = affin[0] + jnp.where(same_xy, affin[1], 0.0) + jnp.where(same_xz, affin[2], 0.0)
    sum_y = affin[1] + jnp.where(same_yz, affin[2], 0.0)
    top_x = sum_x.astype(jnp.bfloat16).astype(jnp.float32)
    top_y = sum_y.astype(jnp.bfloat16).astype(jnp.float32)
    in_x = same_xy | same_xz
    rest = jnp.where(in_x, sum_x - top_x, sum_y - top_y)
    rest_at = jnp.where(in_x, oth_x, oth_y)

    ids = lax.broadcasted_iota(jnp.int32, (LABELS, CZ), 0).astype(jnp.float32).astype(jnp.bfloat16)

    def spread_row(values, y):
        wide = jnp.broadcast_to(values[y : y + 1, :], (16, CZ)).astype(jnp.bfloat16)
        return jnp.concatenate([wide] * (LABELS // 16), axis=0)

    zero = jnp.zeros((LABELS, CZ), jnp.bfloat16)
    one = jnp.ones((LABELS, CZ), jnp.bfloat16)
    lefts, tops, rests = [], [], []
    for y in range(CY):
        lefts.append(jnp.where(spread_row(own, y) == ids, one, zero))
        tops.append(
            jnp.where(
                spread_row(oth_x, y) == ids,
                spread_row(top_x, y),
                jnp.where(
                    spread_row(oth_y, y) == ids,
                    spread_row(top_y, y),
                    jnp.where(spread_row(oth_z, y) == ids, spread_row(affin[2], y), zero),
                ),
            )
        )
        rests.append(jnp.where(spread_row(rest_at, y) == ids, spread_row(rest, y), zero))
    left = jnp.concatenate(lefts, axis=1)
    right = jnp.concatenate(
        [jnp.concatenate(tops, axis=1), jnp.concatenate(rests, axis=1)], axis=0
    )
    found = lax.dot_general(
        right, left, (((1,), (1,)), ((), ())), preferred_element_type=jnp.float32
    )
    return found[:LABELS] + found[LABELS:]


def slot_rows(table, ends_ref, owner_ref, row_ref, count_ref):
    first = ends_ref[0:1, :]
    second = ends_ref[1:2, :]
    label = lax.broadcasted_iota(jnp.int32, (LABELS, SLOTS), 0)
    slot = lax.broadcasted_iota(jnp.int32, (1, SLOTS), 1)
    picked = jnp.dot(
        table + table.T,
        (first == label).astype(jnp.float32),
        precision=lax.Precision.HIGHEST,
        preferred_element_type=jnp.float32,
    )
    value = jnp.sum(jnp.where(second == label, picked, 0.0), axis=0, keepdims=True)
    keep = (slot < count_ref[0]) & (first != second)
    value = jnp.where(keep, value, 0.0)
    owner = owner_ref[...]
    place = (owner & (NBY - 1)) * NBX + (owner >> 4)
    row_id = lax.broadcasted_iota(jnp.int32, (EO, SLOTS), 0)
    return lax.dot_general(
        jnp.where(place == row_id, value, 0.0),
        (row_ref[...] == row_id).astype(jnp.float32),
        (((1,), (1,)), ((), ())),
        precision=lax.Precision.HIGHEST,
        preferred_element_type=jnp.float32,
    )


def whole_kernel(
    f_ref,
    own_ref,
    conv_ref,
    bias_ref,
    head_ref,
    head_bias_ref,
    ends_ref,
    owner_ref,
    row_ref,
    count_ref,
    o_ref,
    fbuf_ref,
    p_ref,
    lab_ref,
    line_ref,
    last_line_ref,
    w_ref,
    logit_ref,
    table_ref,
    rows_ref,
    got_ref,
    mid_ref,
    last_ref,
    load_sem,
    y_send,
    y_recv,
    x_send,
    x_recv,
    send1,
    recv1,
    send2,
    recv2,
):
    bx = lax.axis_index("bx")
    by = lax.axis_index("by")
    xm = lax.rem(bx + NBX - 1, NBX)
    xp = lax.rem(bx + 1, NBX)
    ym = lax.rem(by + NBY - 1, NBY)
    yp = lax.rem(by + 1, NBY)
    barrier = pltpu.get_barrier_semaphore()

    def greet(peer):
        pl.semaphore_signal(barrier, inc=1, device_id=peer, device_id_type=MESH)

    for step in range(1, NBY):
        greet((bx, lax.rem(by + step, NBY)))
    for step in range(1, NBX):
        greet((lax.rem(bx + step, NBX), by))
    for peer in ((xm, ym), (xm, yp), (xp, ym), (xp, yp)):
        greet(peer)

    def load(pair):
        at = pl.ds(2 * pair, 2)
        return pltpu.make_async_copy(f_ref.at[:, at], fbuf_ref.at[:, at], load_sem.at[pair])

    for pair in range(CX // 2):
        load(pair).start()

    lab_ref[1:] = own_ref[...]
    last_line_ref[...] = own_ref[:, CY - 1, :]
    table_ref[...] = jnp.zeros((LABELS, LABELS), jnp.float32)
    lay_weights(conv_ref, w_ref)
    to = lax.broadcasted_iota(jnp.int32, (256, 256), 0)
    come = lax.broadcasted_iota(jnp.int32, (256, 256), 1)
    perm = ((to & 15) * 16 + (to >> 4) == come).astype(jnp.float32).astype(jnp.bfloat16)
    pl.semaphore_wait(barrier, NBX + NBY + 2)

    def remote(src, dst, send_sem, recv_sem, peer):
        return pltpu.make_async_remote_copy(
            src_ref=src,
            dst_ref=dst,
            send_sem=send_sem,
            recv_sem=recv_sem,
            device_id=peer,
            device_id_type=MESH,
        )

    def y_copies(pair):
        at = pl.ds(1 + 2 * pair, 2)
        return (
            remote(
                p_ref.at[at, 1], p_ref.at[at, CY + 1], y_send.at[0, pair], y_recv.at[0, pair], (bx, ym)
            ),
            remote(
                p_ref.at[at, CY], p_ref.at[at, 0], y_send.at[1, pair], y_recv.at[1, pair], (bx, yp)
            ),
        )

    inner = pl.ds(1, CY)
    x_copies = [
        remote(src, dst, x_send.at[n], x_recv.at[n], peer)
        for n, (src, dst, peer) in enumerate(
            [
                (p_ref.at[1, inner], p_ref.at[CX + 1, inner], (xm, by)),
                (p_ref.at[1, 1], p_ref.at[CX + 1, CY + 1], (xm, ym)),
                (p_ref.at[1, CY], p_ref.at[CX + 1, 0], (xm, yp)),
                (p_ref.at[CX, inner], p_ref.at[0, inner], (xp, by)),
                (p_ref.at[CX, 1], p_ref.at[0, CY + 1], (xp, ym)),
                (p_ref.at[CX, CY], p_ref.at[0, 0], (xp, yp)),
                (own_ref.at[CX - 1], lab_ref.at[0], (xp, by)),
                (last_line_ref, line_ref, (bx, yp)),
            ]
        )
    ]

    def turned(n, carry):
        pair = lax.rem(n + CX // 2 - 1, CX // 2)
        load(pair).wait()
        for group in range(C // 16):
            block = jnp.concatenate(
                [
                    fbuf_ref[16 * group : 16 * group + 16, 2 * pair + half].reshape(256, CZ)
                    for half in range(2)
                ],
                axis=1,
            )
            out = jnp.dot(perm, block, preferred_element_type=jnp.float32).astype(jnp.bfloat16)
            for half in range(2):
                p_ref[1 + 2 * pair + half, 1 : CY + 1, 16 * group : 16 * group + 16, :] = out[
                    :, half * CZ : (half + 1) * CZ
                ].reshape(CY, 16, CZ)
        for copy in y_copies(pair):
            copy.start()
        return carry

    lax.fori_loop(0, 2, turned, 0)
    for copy in x_copies:
        copy.start()
    lax.fori_loop(2, CX // 2, turned, 0)
    for copy in x_copies:
        copy.wait()
    for pair in range(CX // 2):
        for copy in y_copies(pair):
            copy.wait()

    @pl.when(bx == 0)
    def _():
        p_ref[0] = jnp.zeros((CY + 2, C, CZ), jnp.bfloat16)
        lab_ref[0] = jnp.full((CY, CZ), -1, jnp.int32)

    @pl.when(bx == NBX - 1)
    def _():
        p_ref[CX + 1] = jnp.zeros((CY + 2, C, CZ), jnp.bfloat16)

    @pl.when(by == 0)
    def _():
        p_ref[:, 0] = jnp.zeros((CX + 2, C, CZ), jnp.bfloat16)
        line_ref[...] = jnp.full((CX, CZ), -1, jnp.int32)

    @pl.when(by == NBY - 1)
    def _():
        p_ref[:, CY + 1] = jnp.zeros((CX + 2, C, CZ), jnp.bfloat16)

    conv_plane(0, p_ref, w_ref, bias_ref, head_ref, head_bias_ref, logit_ref)

    def plane(x, carry):
        found = pair_sums(x - 1, logit_ref, lab_ref, line_ref)
        conv_plane(x, p_ref, w_ref, bias_ref, head_ref, head_bias_ref, logit_ref)
        table_ref[...] += found
        return carry

    lax.fori_loop(1, CX, plane, 0)
    table = table_ref[...] + pair_sums(CX - 1, logit_ref, lab_ref, line_ref)
    rows_ref[...] = slot_rows(table, ends_ref, owner_ref, row_ref, count_ref).reshape(NBY, NBX, EO)

    copies = []
    for step in range(1, NBY):
        to = lax.rem(by + step, NBY)
        copies.append(
            remote(rows_ref.at[to], got_ref.at[step], send1.at[step], recv1.at[step], (bx, to))
        )
        copies[-1].start()
    total = rows_ref[by]
    for step in range(1, NBY):
        copies[step - 1].wait()
        total = total + got_ref[step]
    for row in range(NBX):
        mid_ref[row] = total[row : row + 1, :]
    copies = []
    for step in range(1, NBX):
        to = lax.rem(bx + step, NBX)
        copies.append(
            remote(mid_ref.at[to], last_ref.at[step], send2.at[step], recv2.at[step], (to, by))
        )
        copies[-1].start()
    total = mid_ref[bx]
    for step in range(1, NBX):
        copies[step - 1].wait()
        total = total + last_ref[step]
    o_ref[...] = total


def on_device(
    features,
    labels,
    conv_weight,
    conv_bias,
    head_weight,
    head_bias,
    edge_ends,
    edge_owner,
    edge_row,
    edge_count,
):
    bias = jnp.broadcast_to(jnp.concatenate([conv_bias, conv_bias])[:, None], (2 * C, CZ))
    blank = jnp.zeros((3, C), jnp.bfloat16)
    head = jnp.stack(
        [
            jnp.concatenate([head_weight, blank], axis=1),
            jnp.concatenate([blank, head_weight], axis=1),
        ],
        axis=1,
    ).reshape(6, 2 * C)
    head = jnp.pad(head, ((0, 10), (0, 0)))
    bf16, f32, i32 = jnp.bfloat16, jnp.float32, jnp.int32
    total = pl.pallas_call(
        whole_kernel,
        out_shape=jax.ShapeDtypeStruct((1, EO), f32),
        in_specs=[pl.BlockSpec(memory_space=pl.ANY)] + [VMEM] * 4 + [SMEM] + [VMEM] * 3 + [SMEM],
        out_specs=VMEM,
        scratch_shapes=[
            pltpu.VMEM((C, CX, CY, CZ), bf16),
            pltpu.VMEM((CX + 2, CY + 2, C, CZ), bf16),
            pltpu.VMEM((CX + 1, CY, CZ), i32),
            pltpu.VMEM((CX, CZ), i32),
            pltpu.VMEM((CX, CZ), i32),
            pltpu.VMEM((6 * C, 12 * C), bf16),
            pltpu.VMEM((3, CY, CZ), f32),
            pltpu.VMEM((LABELS, LABELS), f32),
            pltpu.VMEM((NBY, NBX, EO), f32),
            pltpu.VMEM((NBY, NBX, EO), f32),
            pltpu.VMEM((NBX, 1, EO), f32),
            pltpu.VMEM((NBX, 1, EO), f32),
            pltpu.SemaphoreType.DMA((CX // 2,)),
            pltpu.SemaphoreType.DMA((2, CX // 2)),
            pltpu.SemaphoreType.DMA((2, CX // 2)),
            pltpu.SemaphoreType.DMA((8,)),
            pltpu.SemaphoreType.DMA((8,)),
            pltpu.SemaphoreType.DMA((NBY,)),
            pltpu.SemaphoreType.DMA((NBY,)),
            pltpu.SemaphoreType.DMA((NBX,)),
            pltpu.SemaphoreType.DMA((NBX,)),
        ],
        compiler_params=pltpu.CompilerParams(
            collective_id=0, has_side_effects=True, vmem_limit_bytes=52 * 2**20
        ),
        name="whole",
    )(
        features,
        labels,
        conv_weight,
        bias,
        head,
        head_bias,
        edge_ends[0],
        edge_owner[:, :, 0],
        edge_row,
        edge_count,
    )
    return total[0]


def solution(mesh):
    placed = (
        P(None, "bx", "by", None),
        P("bx", "by", None),
        P(),
        P(),
        P(),
        P(),
        P(("bx", "by"), None, None),
        P(("bx", "by"), None, None),
        P(("bx", "by"), None),
        P(("bx", "by")),
    )
    return jax.shard_map(
        on_device, mesh=mesh, in_specs=placed, out_specs=P(("bx", "by")), check_vma=False
    )
```

```python
import jax
import jax.numpy as jnp
from jax import lax
from jax.experimental import pallas as pl
from jax.experimental.pallas import tpu as pltpu
from jax.sharding import PartitionSpec as P

LABELS = 256
EO = 128
NBX = 8
NBY = 16
CX = 16
CY = 16
CZ = 128
C = 64
SLOTS = 512
PAIRS = CY // 2
MESH = pl.DeviceIdType.MESH
VMEM = pl.BlockSpec(memory_space=pltpu.VMEM)


def lay_weights(conv_ref, w_ref):
    blank = jnp.zeros((C, C), jnp.bfloat16)
    for dz in range(3):
        for out_y in range(2):
            pieces = []
            for dx in range(3):
                for in_y in range(4):
                    dy = in_y - out_y
                    at = (9 * dx + 3 * dy + dz) * C
                    pieces.append(conv_ref[:, at : at + C] if 0 <= dy <= 2 else blank)
            w_ref[(2 * dz + out_y) * C : (2 * dz + out_y + 1) * C, :] = jnp.concatenate(
                pieces, axis=1
            )


def conv_plane(x, p_ref, w_ref, bias_ref, head_ref, head_bias_ref, logit_ref):
    lane = lax.broadcasted_iota(jnp.int32, (2 * C, CZ), 1)
    stacked = jnp.concatenate(
        [
            jnp.concatenate(
                [p_ref[x + dx, 2 * j : 2 * j + 4].reshape(4 * C, CZ) for j in range(PAIRS)], axis=1
            )
            for dx in range(3)
        ],
        axis=0,
    )
    sums = jnp.dot(w_ref[...], stacked, preferred_element_type=jnp.float32)
    parts = []
    for j in range(PAIRS):
        part = sums[:, j * CZ : (j + 1) * CZ]
        before = pltpu.roll(part[: 2 * C], 1, 1)
        after = pltpu.roll(part[4 * C :], CZ - 1, 1)
        pre = (
            part[2 * C : 4 * C]
            + jnp.where(lane > 0, before, 0.0)
            + jnp.where(lane < CZ - 1, after, 0.0)
            + bias_ref[...]
        )
        parts.append(jnp.maximum(pre, 0.0).astype(jnp.bfloat16))
    hidden = jnp.concatenate([part[:C] for part in parts] + [part[C:] for part in parts], axis=1)
    logits = jnp.dot(head_ref[...], hidden, preferred_element_type=jnp.float32)
    for d in range(3):
        for y in range(CY):
            at = (y % 2) * PAIRS + y // 2
            logit_ref[d, y : y + 1, :] = (
                logits[d : d + 1, at * CZ : (at + 1) * CZ] + head_bias_ref[d]
            )


def pair_sums(x, logit_ref, lab_ref, line_ref):
    affin = [
        jax.nn.sigmoid(logit_ref[d]).astype(jnp.bfloat16).astype(jnp.float32) for d in range(3)
    ]
    own_i = lab_ref[x + 1]
    line = lax.broadcasted_iota(jnp.int32, (CY, CZ), 0)
    deep = lax.broadcasted_iota(jnp.int32, (CY, CZ), 1)
    edge_line = jnp.broadcast_to(line_ref[pl.ds(x, 1), :], (CY, CZ))
    own = own_i.astype(jnp.float32)
    oth_x = lab_ref[x].astype(jnp.float32)
    oth_y = jnp.where(line > 0, pltpu.roll(own_i, 1, 0), edge_line).astype(jnp.float32)
    oth_z = jnp.where(deep > 0, pltpu.roll(own_i, 1, 1), -1).astype(jnp.float32)
    same_xy = oth_x == oth_y
    same_xz = oth_x == oth_z
    same_yz = oth_y == oth_z
    sum_x = affin[0] + jnp.where(same_xy, affin[1], 0.0) + jnp.where(same_xz, affin[2], 0.0)
    sum_y = affin[1] + jnp.where(same_yz, affin[2], 0.0)
    top_x = sum_x.astype(jnp.bfloat16).astype(jnp.float32)
    top_y = sum_y.astype(jnp.bfloat16).astype(jnp.float32)
    in_x = same_xy | same_xz
    rest = jnp.where(in_x, sum_x - top_x, sum_y - top_y)
    rest_at = jnp.where(in_x, oth_x, oth_y)

    ids = lax.broadcasted_iota(jnp.int32, (LABELS, CZ), 0).astype(jnp.float32).astype(jnp.bfloat16)

    def spread_row(values, y):
        wide = jnp.broadcast_to(values[y : y + 1, :], (16, CZ)).astype(jnp.bfloat16)
        return jnp.concatenate([wide] * (LABELS // 16), axis=0)

    zero = jnp.zeros((LABELS, CZ), jnp.bfloat16)
    one = jnp.ones((LABELS, CZ), jnp.bfloat16)
    lefts, tops, rests = [], [], []
    for y in range(CY):
        lefts.append(jnp.where(spread_row(own, y) == ids, one, zero))
        tops.append(
            jnp.where(
                spread_row(oth_x, y) == ids,
                spread_row(top_x, y),
                jnp.where(
                    spread_row(oth_y, y) == ids,
                    spread_row(top_y, y),
                    jnp.where(spread_row(oth_z, y) == ids, spread_row(affin[2], y), zero),
                ),
            )
        )
        rests.append(jnp.where(spread_row(rest_at, y) == ids, spread_row(rest, y), zero))
    left = jnp.concatenate(lefts, axis=1)
    right = jnp.concatenate(
        [jnp.concatenate(tops, axis=1), jnp.concatenate(rests, axis=1)], axis=0
    )
    found = lax.dot_general(
        right, left, (((1,), (1,)), ((), ())), preferred_element_type=jnp.float32
    )
    return found[:LABELS] + found[LABELS:]


def slot_rows(table, ends_ref, owner_ref, row_ref, count_ref):
    first = ends_ref[0, 0:1, :]
    second = ends_ref[0, 1:2, :]
    label = lax.broadcasted_iota(jnp.int32, (LABELS, SLOTS), 0)
    slot = lax.broadcasted_iota(jnp.int32, (1, SLOTS), 1)
    picked = jnp.dot(
        table + table.T,
        (first == label).astype(jnp.float32),
        precision=lax.Precision.HIGHEST,
        preferred_element_type=jnp.float32,
    )
    value = jnp.sum(jnp.where(second == label, picked, 0.0), axis=0, keepdims=True)
    keep = (slot < count_ref[...]) & (first != second)
    value = jnp.where(keep, value, 0.0)
    owner = owner_ref[...]
    place = (owner & (NBY - 1)) * NBX + (owner >> 4)
    row_id = lax.broadcasted_iota(jnp.int32, (EO, SLOTS), 0)
    return lax.dot_general(
        jnp.where(place == row_id, value, 0.0),
        (row_ref[...] == row_id).astype(jnp.float32),
        (((1,), (1,)), ((), ())),
        precision=lax.Precision.HIGHEST,
        preferred_element_type=jnp.float32,
    )


def whole_kernel(
    f_ref,
    own_hbm,
    conv_hbm,
    row_bias_hbm,
    head_hbm,
    head_bias_hbm,
    ends_hbm,
    owner_hbm,
    row_hbm,
    count_hbm,
    o_ref,
    conv_ref,
    row_bias_ref,
    head_ref,
    head_bias_ref,
    ends_ref,
    owner_ref,
    row_ref,
    count_ref,
    bias_ref,
    fbuf_ref,
    p_ref,
    lab_ref,
    line_ref,
    last_line_ref,
    w_ref,
    logit_ref,
    table_ref,
    rows_ref,
    got_ref,
    mid_ref,
    last_ref,
    small_sem,
    load_sem,
    y_send,
    y_recv,
    x_send,
    x_recv,
    send1,
    recv1,
    send2,
    recv2,
):
    bx = lax.axis_index("bx")
    by = lax.axis_index("by")
    xm = lax.rem(bx + NBX - 1, NBX)
    xp = lax.rem(bx + 1, NBX)
    ym = lax.rem(by + NBY - 1, NBY)
    yp = lax.rem(by + 1, NBY)
    barrier = pltpu.get_barrier_semaphore()

    def greet(peer):
        pl.semaphore_signal(barrier, inc=1, device_id=peer, device_id_type=MESH)

    for step in range(1, NBY):
        greet((bx, lax.rem(by + step, NBY)))
    for step in range(1, NBX):
        greet((lax.rem(bx + step, NBX), by))
    for peer in ((xm, ym), (xm, yp), (xp, ym), (xp, yp)):
        greet(peer)

    def load(pair):
        at = pl.ds(2 * pair, 2)
        return pltpu.make_async_copy(f_ref.at[:, at], fbuf_ref.at[:, at], load_sem.at[pair])

    small = [
        pltpu.make_async_copy(src, dst, small_sem.at[n])
        for n, (src, dst) in enumerate(
            [
                (conv_hbm, conv_ref),
                (own_hbm, lab_ref.at[pl.ds(1, CX)]),
                (row_bias_hbm, row_bias_ref),
                (head_hbm, head_ref),
                (head_bias_hbm, head_bias_ref),
                (ends_hbm, ends_ref),
                (owner_hbm, owner_ref),
                (row_hbm, row_ref),
                (count_hbm, count_ref),
            ]
        )
    ]
    for copy in small:
        copy.start()
    for pair in (7, 0, 1, 2, 3, 4, 5, 6):
        load(pair).start()

    table_ref[...] = jnp.zeros((LABELS, LABELS), jnp.float32)
    for copy in small:
        copy.wait()
    last_line_ref[...] = lab_ref[1:, CY - 1, :]
    diagonal = lax.broadcasted_iota(jnp.int32, (C, C), 0) == lax.broadcasted_iota(
        jnp.int32, (C, C), 1
    )
    column = jnp.sum(jnp.where(diagonal, row_bias_ref[...], 0.0), axis=1, keepdims=True)
    for out_y in range(2):
        bias_ref[out_y * C : (out_y + 1) * C, :] = jnp.broadcast_to(column, (C, CZ))
    lay_weights(conv_ref, w_ref)
    to = lax.broadcasted_iota(jnp.int32, (256, 256), 0)
    come = lax.broadcasted_iota(jnp.int32, (256, 256), 1)
    perm = ((to & 15) * 16 + (to >> 4) == come).astype(jnp.float32).astype(jnp.bfloat16)
    pl.semaphore_wait(barrier, NBX + NBY + 2)

    def remote(src, dst, send_sem, recv_sem, peer):
        return pltpu.make_async_remote_copy(
            src_ref=src,
            dst_ref=dst,
            send_sem=send_sem,
            recv_sem=recv_sem,
            device_id=peer,
            device_id_type=MESH,
        )

    def y_copies(pair):
        at = pl.ds(1 + 2 * pair, 2)
        return (
            remote(
                p_ref.at[at, 1], p_ref.at[at, CY + 1], y_send.at[0, pair], y_recv.at[0, pair], (bx, ym)
            ),
            remote(
                p_ref.at[at, CY], p_ref.at[at, 0], y_send.at[1, pair], y_recv.at[1, pair], (bx, yp)
            ),
        )

    inner = pl.ds(1, CY)
    x_copies = [
        remote(src, dst, x_send.at[n], x_recv.at[n], peer)
        for n, (src, dst, peer) in enumerate(
            [
                (p_ref.at[1, inner], p_ref.at[CX + 1, inner], (xm, by)),
                (p_ref.at[1, 1], p_ref.at[CX + 1, CY + 1], (xm, ym)),
                (p_ref.at[1, CY], p_ref.at[CX + 1, 0], (xm, yp)),
                (p_ref.at[CX, inner], p_ref.at[0, inner], (xp, by)),
                (p_ref.at[CX, 1], p_ref.at[0, CY + 1], (xp, ym)),
                (p_ref.at[CX, CY], p_ref.at[0, 0], (xp, yp)),
                (lab_ref.at[CX], lab_ref.at[0], (xp, by)),
                (last_line_ref, line_ref, (bx, yp)),
            ]
        )
    ]

    def turned(n, carry):
        pair = lax.rem(n + CX // 2 - 1, CX // 2)
        load(pair).wait()
        for group in range(C // 16):
            block = jnp.concatenate(
                [
                    fbuf_ref[16 * group : 16 * group + 16, 2 * pair + half].reshape(256, CZ)
                    for half in range(2)
                ],
                axis=1,
            )
            out = jnp.dot(perm, block, preferred_element_type=jnp.float32).astype(jnp.bfloat16)
            for half in range(2):
                p_ref[1 + 2 * pair + half, 1 : CY + 1, 16 * group : 16 * group + 16, :] = out[
                    :, half * CZ : (half + 1) * CZ
                ].reshape(CY, 16, CZ)
        for copy in y_copies(pair):
            copy.start()
        return carry

    lax.fori_loop(0, 2, turned, 0)
    for copy in x_copies:
        copy.start()
    lax.fori_loop(2, CX // 2, turned, 0)
    for copy in x_copies:
        copy.wait()
    for pair in range(CX // 2):
        for copy in y_copies(pair):
            copy.wait()

    @pl.when(bx == 0)
    def _():
        p_ref[0] = jnp.zeros((CY + 2, C, CZ), jnp.bfloat16)
        lab_ref[0] = jnp.full((CY, CZ), -1, jnp.int32)

    @pl.when(bx == NBX - 1)
    def _():
        p_ref[CX + 1] = jnp.zeros((CY + 2, C, CZ), jnp.bfloat16)

    @pl.when(by == 0)
    def _():
        p_ref[:, 0] = jnp.zeros((CX + 2, C, CZ), jnp.bfloat16)
        line_ref[...] = jnp.full((CX, CZ), -1, jnp.int32)

    @pl.when(by == NBY - 1)
    def _():
        p_ref[:, CY + 1] = jnp.zeros((CX + 2, C, CZ), jnp.bfloat16)

    conv_plane(0, p_ref, w_ref, bias_ref, head_ref, head_bias_ref, logit_ref)

    def plane(x, carry):
        found = pair_sums(x - 1, logit_ref, lab_ref, line_ref)
        conv_plane(x, p_ref, w_ref, bias_ref, head_ref, head_bias_ref, logit_ref)
        table_ref[...] += found
        return carry

    lax.fori_loop(1, CX, plane, 0)
    table = table_ref[...] + pair_sums(CX - 1, logit_ref, lab_ref, line_ref)
    rows_ref[...] = slot_rows(table, ends_ref, owner_ref, row_ref, count_ref).reshape(NBY, NBX, EO)

    copies = []
    for step in range(1, NBY):
        to = lax.rem(by + step, NBY)
        copies.append(
            remote(rows_ref.at[to], got_ref.at[step], send1.at[step], recv1.at[step], (bx, to))
        )
        copies[-1].start()
    total = rows_ref[by]
    for step in range(1, NBY):
        copies[step - 1].wait()
        total = total + got_ref[step]
    for row in range(NBX):
        mid_ref[row] = total[row : row + 1, :]
    copies = []
    for step in range(1, NBX):
        to = lax.rem(bx + step, NBX)
        copies.append(
            remote(mid_ref.at[to], last_ref.at[step], send2.at[step], recv2.at[step], (to, by))
        )
        copies[-1].start()
    total = mid_ref[bx]
    for step in range(1, NBX):
        copies[step - 1].wait()
        total = total + last_ref[step]
    o_ref[...] = total


def on_device(
    features,
    labels,
    conv_weight,
    conv_bias,
    head_weight,
    head_bias,
    edge_ends,
    edge_owner,
    edge_row,
    edge_count,
):
    bf16, f32, i32 = jnp.bfloat16, jnp.float32, jnp.int32
    total = pl.pallas_call(
        whole_kernel,
        out_shape=jax.ShapeDtypeStruct((1, EO), f32),
        in_specs=[pl.BlockSpec(memory_space=pl.ANY)] * 10,
        out_specs=VMEM,
        scratch_shapes=[
            pltpu.VMEM((C, 27 * C), bf16),
            pltpu.VMEM((1, C), f32),
            pltpu.VMEM((3, C), bf16),
            pltpu.SMEM((3,), f32),
            pltpu.VMEM((1, 2, SLOTS), i32),
            pltpu.VMEM((1, SLOTS), i32),
            pltpu.VMEM((1, SLOTS), i32),
            pltpu.VMEM((1, 1), i32),
            pltpu.VMEM((2 * C, CZ), f32),
            pltpu.VMEM((C, CX, CY, CZ), bf16),
            pltpu.VMEM((CX + 2, CY + 2, C, CZ), bf16),
            pltpu.VMEM((CX + 1, CY, CZ), i32),
            pltpu.VMEM((CX, CZ), i32),
            pltpu.VMEM((CX, CZ), i32),
            pltpu.VMEM((6 * C, 12 * C), bf16),
            pltpu.VMEM((3, CY, CZ), f32),
            pltpu.VMEM((LABELS, LABELS), f32),
            pltpu.VMEM((NBY, NBX, EO), f32),
            pltpu.VMEM((NBY, NBX, EO), f32),
            pltpu.VMEM((NBX, 1, EO), f32),
            pltpu.VMEM((NBX, 1, EO), f32),
            pltpu.SemaphoreType.DMA((9,)),
            pltpu.SemaphoreType.DMA((CX // 2,)),
            pltpu.SemaphoreType.DMA((2, CX // 2)),
            pltpu.SemaphoreType.DMA((2, CX // 2)),
            pltpu.SemaphoreType.DMA((8,)),
            pltpu.SemaphoreType.DMA((8,)),
            pltpu.SemaphoreType.DMA((NBY,)),
            pltpu.SemaphoreType.DMA((NBY,)),
            pltpu.SemaphoreType.DMA((NBX,)),
            pltpu.SemaphoreType.DMA((NBX,)),
        ],
        compiler_params=pltpu.CompilerParams(
            collective_id=0, has_side_effects=True, vmem_limit_bytes=63 * 2**20
        ),
        name="whole",
    )(
        features,
        labels,
        conv_weight,
        conv_bias[None],
        head_weight,
        head_bias,
        edge_ends,
        edge_owner[:, :, 0],
        edge_row,
        edge_count[None],
    )
    return total[0]


def solution(mesh):
    placed = (
        P(None, "bx", "by", None),
        P("bx", "by", None),
        P(),
        P(),
        P(),
        P(),
        P(("bx", "by"), None, None),
        P(("bx", "by"), None, None),
        P(("bx", "by"), None),
        P(("bx", "by")),
    )
    return jax.shard_map(
        on_device, mesh=mesh, in_specs=placed, out_specs=P(("bx", "by")), check_vma=False
    )
```

```python
import jax
import jax.numpy as jnp
from jax import lax
from jax.experimental import pallas as pl
from jax.experimental.pallas import tpu as pltpu
from jax.sharding import PartitionSpec as P

LABELS = 256
EO = 128
NBX = 8
NBY = 16
CX = 16
CY = 16
CZ = 128
C = 64
SLOTS = 512
PAIRS = CY // 2
EARLY = 8
DEVICES = NBX * NBY
MESH = pl.DeviceIdType.MESH
VMEM = pl.BlockSpec(memory_space=pltpu.VMEM)


def lay_weights(conv_ref, w_ref):
    blank = jnp.zeros((C, C), jnp.bfloat16)
    for dz in range(3):
        for out_y in range(2):
            pieces = []
            for dx in range(3):
                for in_y in range(4):
                    dy = in_y - out_y
                    at = (9 * dx + 3 * dy + dz) * C
                    pieces.append(conv_ref[:, at : at + C] if 0 <= dy <= 2 else blank)
            w_ref[(2 * dz + out_y) * C : (2 * dz + out_y + 1) * C, :] = jnp.concatenate(
                pieces, axis=1
            )


def conv_pairs(pairs, p_ref, w_ref, bias_ref, head_ref, head_bias_ref, logit_ref):
    lane = lax.broadcasted_iota(jnp.int32, (2 * C, CZ), 1)
    stacked = jnp.concatenate(
        [
            jnp.concatenate(
                [p_ref[x + dx, 2 * j : 2 * j + 4].reshape(4 * C, CZ) for x, j in pairs], axis=1
            )
            for dx in range(3)
        ],
        axis=0,
    )
    sums = jnp.dot(w_ref[...], stacked, preferred_element_type=jnp.float32)
    parts = []
    for n in range(len(pairs)):
        part = sums[:, n * CZ : (n + 1) * CZ]
        before = pltpu.roll(part[: 2 * C], 1, 1)
        after = pltpu.roll(part[4 * C :], CZ - 1, 1)
        pre = (
            part[2 * C : 4 * C]
            + jnp.where(lane > 0, before, 0.0)
            + jnp.where(lane < CZ - 1, after, 0.0)
            + bias_ref[...]
        )
        parts.append(jnp.maximum(pre, 0.0).astype(jnp.bfloat16))
    hidden = jnp.concatenate([part[:C] for part in parts] + [part[C:] for part in parts], axis=1)
    logits = jnp.dot(head_ref[...], hidden, preferred_element_type=jnp.float32)
    for d in range(3):
        for n, (x, j) in enumerate(pairs):
            for out_y in range(2):
                at = out_y * len(pairs) + n
                y = 2 * j + out_y
                logit_ref[x, d, y : y + 1, :] = (
                    logits[d : d + 1, at * CZ : (at + 1) * CZ] + head_bias_ref[d]
                )


def pair_sums(x, logit_ref, lab_ref, line_ref):
    affin = [
        jax.nn.sigmoid(logit_ref[x, d]).astype(jnp.bfloat16).astype(jnp.float32) for d in range(3)
    ]
    own_i = lab_ref[x + 1]
    line = lax.broadcasted_iota(jnp.int32, (CY, CZ), 0)
    deep = lax.broadcasted_iota(jnp.int32, (CY, CZ), 1)
    edge_line = jnp.broadcast_to(line_ref[pl.ds(x, 1), :], (CY, CZ))
    own = own_i.astype(jnp.float32)
    oth_x = lab_ref[x].astype(jnp.float32)
    oth_y = jnp.where(line > 0, pltpu.roll(own_i, 1, 0), edge_line).astype(jnp.float32)
    oth_z = jnp.where(deep > 0, pltpu.roll(own_i, 1, 1), -1).astype(jnp.float32)
    same_xy = oth_x == oth_y
    same_xz = oth_x == oth_z
    same_yz = oth_y == oth_z
    sum_x = affin[0] + jnp.where(same_xy, affin[1], 0.0) + jnp.where(same_xz, affin[2], 0.0)
    sum_y = affin[1] + jnp.where(same_yz, affin[2], 0.0)
    top_x = sum_x.astype(jnp.bfloat16).astype(jnp.float32)
    top_y = sum_y.astype(jnp.bfloat16).astype(jnp.float32)
    in_x = same_xy | same_xz
    rest = jnp.where(in_x, sum_x - top_x, sum_y - top_y)
    rest_at = jnp.where(in_x, oth_x, oth_y)

    ids = lax.broadcasted_iota(jnp.int32, (LABELS, CZ), 0).astype(jnp.float32).astype(jnp.bfloat16)

    def spread_row(values, y):
        wide = jnp.broadcast_to(values[y : y + 1, :], (16, CZ)).astype(jnp.bfloat16)
        return jnp.concatenate([wide] * (LABELS // 16), axis=0)

    zero = jnp.zeros((LABELS, CZ), jnp.bfloat16)
    one = jnp.ones((LABELS, CZ), jnp.bfloat16)
    lefts, tops, rests = [], [], []
    for y in range(CY):
        lefts.append(jnp.where(spread_row(own, y) == ids, one, zero))
        tops.append(
            jnp.where(
                spread_row(oth_x, y) == ids,
                spread_row(top_x, y),
                jnp.where(
                    spread_row(oth_y, y) == ids,
                    spread_row(top_y, y),
                    jnp.where(spread_row(oth_z, y) == ids, spread_row(affin[2], y), zero),
                ),
            )
        )
        rests.append(jnp.where(spread_row(rest_at, y) == ids, spread_row(rest, y), zero))
    left = jnp.concatenate(lefts, axis=1)
    right = jnp.concatenate(
        [jnp.concatenate(tops, axis=1), jnp.concatenate(rests, axis=1)], axis=0
    )
    found = lax.dot_general(
        right, left, (((1,), (1,)), ((), ())), preferred_element_type=jnp.float32
    )
    return found[:LABELS] + found[LABELS:]


def two_terms(value, axis):
    top = value.astype(jnp.bfloat16)
    rest = (value - top.astype(jnp.float32)).astype(jnp.bfloat16)
    return jnp.concatenate([top, rest], axis=axis)


def one_hot(mask):
    return jnp.where(mask, 1.0, 0.0).astype(jnp.bfloat16)


def slot_rows(table, ends_ref, owner_ref, row_ref, count_ref):
    first = ends_ref[0, 0:1, :]
    second = ends_ref[0, 1:2, :]
    label = lax.broadcasted_iota(jnp.int32, (LABELS, SLOTS), 0)
    slot = lax.broadcasted_iota(jnp.int32, (1, SLOTS), 1)
    both = table + table.T
    picked = jnp.dot(
        two_terms(both, 0), one_hot(first == label), preferred_element_type=jnp.float32
    )
    picked = picked[:LABELS] + picked[LABELS:]
    value = jnp.sum(jnp.where(second == label, picked, 0.0), axis=0, keepdims=True)
    keep = (slot < count_ref[...]) & (first != second)
    value = jnp.where(keep, value, 0.0)
    row_id = lax.broadcasted_iota(jnp.int32, (EO, SLOTS), 0)
    spread = lax.dot_general(
        two_terms(jnp.where(owner_ref[...] == row_id, value, 0.0), 0),
        one_hot(row_ref[...] == row_id),
        (((1,), (1,)), ((), ())),
        preferred_element_type=jnp.float32,
    )
    return spread[:EO] + spread[EO:]


def whole_kernel(
    f_ref,
    own_hbm,
    conv_hbm,
    row_bias_hbm,
    head_hbm,
    head_bias_hbm,
    ends_hbm,
    owner_hbm,
    row_hbm,
    count_hbm,
    o_ref,
    conv_ref,
    row_bias_ref,
    head_ref,
    head_bias_ref,
    ends_ref,
    owner_ref,
    row_ref,
    count_ref,
    bias_ref,
    fbuf_ref,
    p_ref,
    lab_ref,
    line_ref,
    last_line_ref,
    w_ref,
    logit_ref,
    table_ref,
    rows_ref,
    got_ref,
    small_sem,
    load_sem,
    y_send,
    y_recv,
    x_send,
    x_recv,
    row_send,
    row_recv,
):
    bx = lax.axis_index("bx")
    by = lax.axis_index("by")
    xm = lax.rem(bx + NBX - 1, NBX)
    xp = lax.rem(bx + 1, NBX)
    ym = lax.rem(by + NBY - 1, NBY)
    yp = lax.rem(by + 1, NBY)
    me = bx * NBY + by
    barrier = pltpu.get_barrier_semaphore()

    def place_of(flat):
        return (flat // NBY, lax.rem(flat, NBY))

    def greet(step, carry):
        peer = place_of(lax.rem(me + step, DEVICES))
        pl.semaphore_signal(barrier, inc=1, device_id=peer, device_id_type=MESH)
        return carry

    def load(pair):
        at = pl.ds(2 * pair, 2)
        return pltpu.make_async_copy(f_ref.at[:, at], fbuf_ref.at[:, at], load_sem.at[pair])

    small = [
        pltpu.make_async_copy(src, dst, small_sem.at[n])
        for n, (src, dst) in enumerate(
            [
                (conv_hbm, conv_ref),
                (own_hbm, lab_ref.at[pl.ds(1, CX)]),
                (row_bias_hbm, row_bias_ref),
                (head_hbm, head_ref),
                (head_bias_hbm, head_bias_ref),
                (ends_hbm, ends_ref),
                (owner_hbm, owner_ref),
                (row_hbm, row_ref),
                (count_hbm, count_ref),
            ]
        )
    ]
    for copy in small:
        copy.start()
    for pair in (7, 0, 1, 2, 3, 4, 5, 6):
        load(pair).start()

    lax.fori_loop(1, DEVICES, greet, 0)
    table_ref[...] = jnp.zeros((LABELS, LABELS), jnp.float32)
    for copy in small:
        copy.wait()
    last_line_ref[...] = lab_ref[1:, CY - 1, :]
    diagonal = lax.broadcasted_iota(jnp.int32, (C, C), 0) == lax.broadcasted_iota(
        jnp.int32, (C, C), 1
    )
    column = jnp.sum(jnp.where(diagonal, row_bias_ref[...], 0.0), axis=1, keepdims=True)
    for out_y in range(2):
        bias_ref[out_y * C : (out_y + 1) * C, :] = jnp.broadcast_to(column, (C, CZ))
    lay_weights(conv_ref, w_ref)
    to = lax.broadcasted_iota(jnp.int32, (256, 256), 0)
    come = lax.broadcasted_iota(jnp.int32, (256, 256), 1)
    perm = ((to & 15) * 16 + (to >> 4) == come).astype(jnp.float32).astype(jnp.bfloat16)
    pl.semaphore_wait(barrier, DEVICES - 1)

    def remote(src, dst, send_sem, recv_sem, peer):
        return pltpu.make_async_remote_copy(
            src_ref=src,
            dst_ref=dst,
            send_sem=send_sem,
            recv_sem=recv_sem,
            device_id=peer,
            device_id_type=MESH,
        )

    def y_copies(pair):
        at = pl.ds(1 + 2 * pair, 2)
        return (
            remote(
                p_ref.at[at, 1], p_ref.at[at, CY + 1], y_send.at[0, pair], y_recv.at[0, pair], (bx, ym)
            ),
            remote(
                p_ref.at[at, CY], p_ref.at[at, 0], y_send.at[1, pair], y_recv.at[1, pair], (bx, yp)
            ),
        )

    inner = pl.ds(1, CY)
    x_copies = [
        remote(src, dst, x_send.at[n], x_recv.at[n], peer)
        for n, (src, dst, peer) in enumerate(
            [
                (p_ref.at[1, inner], p_ref.at[CX + 1, inner], (xm, by)),
                (p_ref.at[1, 1], p_ref.at[CX + 1, CY + 1], (xm, ym)),
                (p_ref.at[1, CY], p_ref.at[CX + 1, 0], (xm, yp)),
                (p_ref.at[CX, inner], p_ref.at[0, inner], (xp, by)),
                (p_ref.at[CX, 1], p_ref.at[0, CY + 1], (xp, ym)),
                (p_ref.at[CX, CY], p_ref.at[0, 0], (xp, yp)),
                (lab_ref.at[CX], lab_ref.at[0], (xp, by)),
                (last_line_ref, line_ref, (bx, yp)),
            ]
        )
    ]

    def turned(n, carry):
        pair = lax.rem(n + CX // 2 - 1, CX // 2)
        load(pair).wait()
        for group in range(C // 16):
            block = jnp.concatenate(
                [
                    fbuf_ref[16 * group : 16 * group + 16, 2 * pair + half].reshape(256, CZ)
                    for half in range(2)
                ],
                axis=1,
            )
            out = jnp.dot(perm, block, preferred_element_type=jnp.float32).astype(jnp.bfloat16)
            for half in range(2):
                p_ref[1 + 2 * pair + half, 1 : CY + 1, 16 * group : 16 * group + 16, :] = out[
                    :, half * CZ : (half + 1) * CZ
                ].reshape(CY, 16, CZ)
        for copy in y_copies(pair):
            copy.start()
        return carry

    lax.fori_loop(0, 2, turned, 0)
    for copy in x_copies:
        copy.start()
    lax.fori_loop(2, CX // 2, turned, 0)

    def early(n, carry):
        pairs = [(1 + 2 * n + m, j) for m in range(2) for j in range(1, PAIRS - 1)]
        conv_pairs(pairs, p_ref, w_ref, bias_ref, head_ref, head_bias_ref, logit_ref)
        return carry

    lax.fori_loop(0, EARLY // 2, early, 0)
    for copy in x_copies:
        copy.wait()
    for pair in range(CX // 2):
        for copy in y_copies(pair):
            copy.wait()

    @pl.when(bx == 0)
    def _():
        p_ref[0] = jnp.zeros((CY + 2, C, CZ), jnp.bfloat16)
        lab_ref[0] = jnp.full((CY, CZ), -1, jnp.int32)

    @pl.when(bx == NBX - 1)
    def _():
        p_ref[CX + 1] = jnp.zeros((CY + 2, C, CZ), jnp.bfloat16)

    @pl.when(by == 0)
    def _():
        p_ref[:, 0] = jnp.zeros((CX + 2, C, CZ), jnp.bfloat16)
        line_ref[...] = jnp.full((CX, CZ), -1, jnp.int32)

    @pl.when(by == NBY - 1)
    def _():
        p_ref[:, CY + 1] = jnp.zeros((CX + 2, C, CZ), jnp.bfloat16)

    for half in range(2):
        pairs = [(1 + 4 * half + n, j) for n in range(4) for j in (0, PAIRS - 1)]
        conv_pairs(pairs, p_ref, w_ref, bias_ref, head_ref, head_bias_ref, logit_ref)

    def plane(n, carry):
        x = lax.rem(n + EARLY + 1, CX)
        found = pair_sums(n + 1, logit_ref, lab_ref, line_ref)
        pairs = [(x, j) for j in range(PAIRS)]
        conv_pairs(pairs, p_ref, w_ref, bias_ref, head_ref, head_bias_ref, logit_ref)
        table_ref[...] += found
        return carry

    lax.fori_loop(0, CX - EARLY, plane, 0)

    def late(n, carry):
        x = lax.rem(n + EARLY + 1, CX)
        table_ref[...] += pair_sums(x, logit_ref, lab_ref, line_ref)
        return carry

    lax.fori_loop(0, CX - EARLY, late, 0)
    rows = slot_rows(table_ref[...], ends_ref, owner_ref, row_ref, count_ref)
    for n in range(EO):
        rows_ref[n] = rows[n : n + 1, :]

    def give(step, carry):
        to = lax.rem(me + step, DEVICES)
        remote(rows_ref.at[to], got_ref.at[step], row_send, row_recv, place_of(to)).start()
        return carry

    lax.fori_loop(1, DEVICES, give, 0)
    others = pl.ds(1, DEVICES - 1)
    remote(
        rows_ref.at[others], got_ref.at[others], row_send, row_recv, place_of(lax.rem(me + 1, DEVICES))
    ).wait()
    totals = [rows_ref[me], got_ref[1], got_ref[2], got_ref[3]]
    for step in range(4, DEVICES):
        totals[step % 4] = totals[step % 4] + got_ref[step]
    total = (totals[0] + totals[1]) + (totals[2] + totals[3])
    o_ref[...] = total


def on_device(
    features,
    labels,
    conv_weight,
    conv_bias,
    head_weight,
    head_bias,
    edge_ends,
    edge_owner,
    edge_row,
    edge_count,
):
    bf16, f32, i32 = jnp.bfloat16, jnp.float32, jnp.int32
    total = pl.pallas_call(
        whole_kernel,
        out_shape=jax.ShapeDtypeStruct((1, EO), f32),
        in_specs=[pl.BlockSpec(memory_space=pl.ANY)] * 10,
        out_specs=VMEM,
        scratch_shapes=[
            pltpu.VMEM((C, 27 * C), bf16),
            pltpu.VMEM((1, C), f32),
            pltpu.VMEM((3, C), bf16),
            pltpu.SMEM((3,), f32),
            pltpu.VMEM((1, 2, SLOTS), i32),
            pltpu.VMEM((1, SLOTS), i32),
            pltpu.VMEM((1, SLOTS), i32),
            pltpu.VMEM((1, 1), i32),
            pltpu.VMEM((2 * C, CZ), f32),
            pltpu.VMEM((C, CX, CY, CZ), bf16),
            pltpu.VMEM((CX + 2, CY + 2, C, CZ), bf16),
            pltpu.VMEM((CX + 1, CY, CZ), i32),
            pltpu.VMEM((CX, CZ), i32),
            pltpu.VMEM((CX, CZ), i32),
            pltpu.VMEM((6 * C, 12 * C), bf16),
            pltpu.VMEM((CX, 3, CY, CZ), f32),
            pltpu.VMEM((LABELS, LABELS), f32),
            pltpu.VMEM((DEVICES, 1, EO), f32),
            pltpu.VMEM((DEVICES, 1, EO), f32),
            pltpu.SemaphoreType.DMA((9,)),
            pltpu.SemaphoreType.DMA((CX // 2,)),
            pltpu.SemaphoreType.DMA((2, CX // 2)),
            pltpu.SemaphoreType.DMA((2, CX // 2)),
            pltpu.SemaphoreType.DMA((8,)),
            pltpu.SemaphoreType.DMA((8,)),
            pltpu.SemaphoreType.DMA,
            pltpu.SemaphoreType.DMA,
        ],
        compiler_params=pltpu.CompilerParams(
            collective_id=0, has_side_effects=True, vmem_limit_bytes=63 * 2**20
        ),
        name="whole",
    )(
        features,
        labels,
        conv_weight,
        conv_bias[None],
        head_weight,
        head_bias,
        edge_ends,
        edge_owner[:, :, 0],
        edge_row,
        edge_count[None],
    )
    return total[0]


def solution(mesh):
    placed = (
        P(None, "bx", "by", None),
        P("bx", "by", None),
        P(),
        P(),
        P(),
        P(),
        P(("bx", "by"), None, None),
        P(("bx", "by"), None, None),
        P(("bx", "by"), None),
        P(("bx", "by")),
    )
    return jax.shard_map(
        on_device, mesh=mesh, in_specs=placed, out_specs=P(("bx", "by")), check_vma=False
    )
```

```python
import jax
import jax.numpy as jnp
from jax import lax
from jax.experimental import pallas as pl
from jax.experimental.pallas import tpu as pltpu
from jax.sharding import PartitionSpec as P

LABELS = 256
EO = 128
NBX = 8
NBY = 16
CX = 16
CY = 16
CZ = 128
C = 64
SLOTS = 512
PAIRS = CY // 2
EARLY = 8
DEVICES = NBX * NBY
MESH = pl.DeviceIdType.MESH
VMEM = pl.BlockSpec(memory_space=pltpu.VMEM)


def lay_weights(conv_ref, w_ref):
    blank = jnp.zeros((C, C), jnp.bfloat16)
    for dz in range(3):
        for out_y in range(2):
            pieces = []
            for dx in range(3):
                for in_y in range(4):
                    dy = in_y - out_y
                    at = (9 * dx + 3 * dy + dz) * C
                    pieces.append(conv_ref[:, at : at + C] if 0 <= dy <= 2 else blank)
            w_ref[(2 * dz + out_y) * C : (2 * dz + out_y + 1) * C, :] = jnp.concatenate(
                pieces, axis=1
            )


def conv_dot(pairs, p_ref, w_ref, sums_ref):
    stacked = jnp.concatenate(
        [
            jnp.concatenate(
                [p_ref[x + dx, 2 * j : 2 * j + 4].reshape(4 * C, CZ) for x, _, j in pairs], axis=1
            )
            for dx in range(3)
        ],
        axis=0,
    )
    sums_ref[:, : len(pairs) * CZ] = jnp.dot(
        w_ref[...], stacked, preferred_element_type=jnp.float32
    )


def conv_head(pairs, sums_ref, bias_ref, head_ref, head_bias_ref, logit_ref):
    lane = lax.broadcasted_iota(jnp.int32, (2 * C, CZ), 1)
    parts = []
    for n in range(len(pairs)):
        part = sums_ref[:, n * CZ : (n + 1) * CZ]
        before = pltpu.roll(part[: 2 * C], 1, 1)
        after = pltpu.roll(part[4 * C :], CZ - 1, 1)
        pre = (
            part[2 * C : 4 * C]
            + jnp.where(lane > 0, before, 0.0)
            + jnp.where(lane < CZ - 1, after, 0.0)
            + bias_ref[...]
        )
        parts.append(jnp.maximum(pre, 0.0).astype(jnp.bfloat16))
    hidden = jnp.concatenate([part[:C] for part in parts] + [part[C:] for part in parts], axis=1)
    logits = jnp.dot(head_ref[...], hidden, preferred_element_type=jnp.float32)
    for d in range(3):
        for n, (_, at, j) in enumerate(pairs):
            for out_y in range(2):
                col = (out_y * len(pairs) + n) * CZ
                y = 2 * j + out_y
                logit_ref[at, d, y : y + 1, :] = logits[d : d + 1, col : col + CZ] + head_bias_ref[d]


def pair_sums(x, at, logit_ref, lab_ref, line_ref):
    affin = [
        jax.nn.sigmoid(logit_ref[at, d]).astype(jnp.bfloat16).astype(jnp.float32) for d in range(3)
    ]
    own_i = lab_ref[x + 1]
    line = lax.broadcasted_iota(jnp.int32, (CY, CZ), 0)
    deep = lax.broadcasted_iota(jnp.int32, (CY, CZ), 1)
    edge_line = jnp.broadcast_to(line_ref[pl.ds(x, 1), :], (CY, CZ))
    own = own_i.astype(jnp.float32)
    oth_x = lab_ref[x].astype(jnp.float32)
    oth_y = jnp.where(line > 0, pltpu.roll(own_i, 1, 0), edge_line).astype(jnp.float32)
    oth_z = jnp.where(deep > 0, pltpu.roll(own_i, 1, 1), -1).astype(jnp.float32)
    same_xy = oth_x == oth_y
    same_xz = oth_x == oth_z
    same_yz = oth_y == oth_z
    sum_x = affin[0] + jnp.where(same_xy, affin[1], 0.0) + jnp.where(same_xz, affin[2], 0.0)
    sum_y = affin[1] + jnp.where(same_yz, affin[2], 0.0)
    top_x = sum_x.astype(jnp.bfloat16).astype(jnp.float32)
    top_y = sum_y.astype(jnp.bfloat16).astype(jnp.float32)
    in_x = same_xy | same_xz
    rest = jnp.where(in_x, sum_x - top_x, sum_y - top_y)
    rest_at = jnp.where(in_x, oth_x, oth_y)

    ids = lax.broadcasted_iota(jnp.int32, (LABELS, CZ), 0).astype(jnp.float32).astype(jnp.bfloat16)

    def spread_row(values, y):
        wide = jnp.broadcast_to(values[y : y + 1, :], (16, CZ)).astype(jnp.bfloat16)
        return jnp.concatenate([wide] * (LABELS // 16), axis=0)

    zero = jnp.zeros((LABELS, CZ), jnp.bfloat16)
    one = jnp.ones((LABELS, CZ), jnp.bfloat16)
    lefts, tops, rests = [], [], []
    for y in range(CY):
        lefts.append(jnp.where(spread_row(own, y) == ids, one, zero))
        tops.append(
            jnp.where(
                spread_row(oth_x, y) == ids,
                spread_row(top_x, y),
                jnp.where(
                    spread_row(oth_y, y) == ids,
                    spread_row(top_y, y),
                    jnp.where(spread_row(oth_z, y) == ids, spread_row(affin[2], y), zero),
                ),
            )
        )
        rests.append(jnp.where(spread_row(rest_at, y) == ids, spread_row(rest, y), zero))
    left = jnp.concatenate(lefts, axis=1)
    right = jnp.concatenate(
        [jnp.concatenate(tops, axis=1), jnp.concatenate(rests, axis=1)], axis=0
    )
    found = lax.dot_general(
        right, left, (((1,), (1,)), ((), ())), preferred_element_type=jnp.float32
    )
    return found[:LABELS] + found[LABELS:]


def two_terms(value, axis):
    top = value.astype(jnp.bfloat16)
    rest = (value - top.astype(jnp.float32)).astype(jnp.bfloat16)
    return jnp.concatenate([top, rest], axis=axis)


def one_hot(mask):
    return jnp.where(mask, 1.0, 0.0).astype(jnp.bfloat16)


def slot_rows(table, ends_ref, owner_ref, row_ref, count_ref):
    first = ends_ref[0, 0:1, :]
    second = ends_ref[0, 1:2, :]
    label = lax.broadcasted_iota(jnp.int32, (LABELS, SLOTS), 0)
    slot = lax.broadcasted_iota(jnp.int32, (1, SLOTS), 1)
    both = table + table.T
    picked = jnp.dot(
        two_terms(both, 0), one_hot(first == label), preferred_element_type=jnp.float32
    )
    picked = picked[:LABELS] + picked[LABELS:]
    value = jnp.sum(jnp.where(second == label, picked, 0.0), axis=0, keepdims=True)
    keep = (slot < count_ref[...]) & (first != second)
    value = jnp.where(keep, value, 0.0)
    row_id = lax.broadcasted_iota(jnp.int32, (EO, SLOTS), 0)
    spread = lax.dot_general(
        two_terms(jnp.where(owner_ref[...] == row_id, value, 0.0), 0),
        one_hot(row_ref[...] == row_id),
        (((1,), (1,)), ((), ())),
        preferred_element_type=jnp.float32,
    )
    return spread[:EO] + spread[EO:]


def whole_kernel(
    f_ref,
    own_hbm,
    conv_hbm,
    row_bias_hbm,
    head_hbm,
    head_bias_hbm,
    ends_hbm,
    owner_hbm,
    row_hbm,
    count_hbm,
    o_ref,
    conv_ref,
    row_bias_ref,
    head_ref,
    head_bias_ref,
    ends_ref,
    owner_ref,
    row_ref,
    count_ref,
    bias_ref,
    fbuf_ref,
    p_ref,
    lab_ref,
    line_ref,
    last_line_ref,
    w_ref,
    logit_a,
    logit_b,
    sums_a,
    sums_b,
    table_ref,
    rows_ref,
    got_ref,
    small_sem,
    load_sem,
    y_send,
    y_recv,
    x_send,
    x_recv,
    row_send,
    row_recv,
):
    bx = lax.axis_index("bx")
    by = lax.axis_index("by")
    xm = lax.rem(bx + NBX - 1, NBX)
    xp = lax.rem(bx + 1, NBX)
    ym = lax.rem(by + NBY - 1, NBY)
    yp = lax.rem(by + 1, NBY)
    me = bx * NBY + by
    barrier = pltpu.get_barrier_semaphore()

    lines = [lax.rem(by + step, NBY) for step in range(NBY)]

    def all_peers(visit):
        def one_x(step, carry):
            peer_x = lax.rem(bx + step, NBX)
            for n in range(NBY):
                visit(peer_x, lines[n], step * NBY + n)
            return carry

        for n in range(1, NBY):
            visit(bx, lines[n], n)
        lax.fori_loop(1, NBX, one_x, 0)

    def greet(peer_x, peer_y, slot):
        pl.semaphore_signal(barrier, inc=1, device_id=(peer_x, peer_y), device_id_type=MESH)

    def load(pair):
        at = pl.ds(2 * pair, 2)
        return pltpu.make_async_copy(f_ref.at[:, at], fbuf_ref.at[:, at], load_sem.at[pair])

    small = [
        pltpu.make_async_copy(src, dst, small_sem.at[n])
        for n, (src, dst) in enumerate(
            [
                (conv_hbm, conv_ref),
                (own_hbm, lab_ref.at[pl.ds(1, CX)]),
                (row_bias_hbm, row_bias_ref),
                (head_hbm, head_ref),
                (head_bias_hbm, head_bias_ref),
                (ends_hbm, ends_ref),
                (owner_hbm, owner_ref),
                (row_hbm, row_ref),
                (count_hbm, count_ref),
            ]
        )
    ]
    for copy in small:
        copy.start()
    for pair in (7, 0, 1, 2, 3, 4, 5, 6):
        load(pair).start()

    all_peers(greet)
    table_ref[...] = jnp.zeros((LABELS, LABELS), jnp.float32)
    for copy in small:
        copy.wait()
    last_line_ref[...] = lab_ref[1:, CY - 1, :]
    diagonal = lax.broadcasted_iota(jnp.int32, (C, C), 0) == lax.broadcasted_iota(
        jnp.int32, (C, C), 1
    )
    column = jnp.sum(jnp.where(diagonal, row_bias_ref[...], 0.0), axis=1, keepdims=True)
    for out_y in range(2):
        bias_ref[out_y * C : (out_y + 1) * C, :] = jnp.broadcast_to(column, (C, CZ))
    lay_weights(conv_ref, w_ref)
    to = lax.broadcasted_iota(jnp.int32, (256, 256), 0)
    come = lax.broadcasted_iota(jnp.int32, (256, 256), 1)
    perm = ((to & 15) * 16 + (to >> 4) == come).astype(jnp.float32).astype(jnp.bfloat16)
    pl.semaphore_wait(barrier, DEVICES - 1)

    def remote(src, dst, send_sem, recv_sem, peer):
        return pltpu.make_async_remote_copy(
            src_ref=src,
            dst_ref=dst,
            send_sem=send_sem,
            recv_sem=recv_sem,
            device_id=peer,
            device_id_type=MESH,
        )

    def y_copies(pair):
        at = pl.ds(1 + 2 * pair, 2)
        return (
            remote(
                p_ref.at[at, 1], p_ref.at[at, CY + 1], y_send.at[0, pair], y_recv.at[0, pair], (bx, ym)
            ),
            remote(
                p_ref.at[at, CY], p_ref.at[at, 0], y_send.at[1, pair], y_recv.at[1, pair], (bx, yp)
            ),
        )

    inner = pl.ds(1, CY)
    x_copies = [
        remote(src, dst, x_send.at[n], x_recv.at[n], peer)
        for n, (src, dst, peer) in enumerate(
            [
                (p_ref.at[1, inner], p_ref.at[CX + 1, inner], (xm, by)),
                (p_ref.at[1, 1], p_ref.at[CX + 1, CY + 1], (xm, ym)),
                (p_ref.at[1, CY], p_ref.at[CX + 1, 0], (xm, yp)),
                (p_ref.at[CX, inner], p_ref.at[0, inner], (xp, by)),
                (p_ref.at[CX, 1], p_ref.at[0, CY + 1], (xp, ym)),
                (p_ref.at[CX, CY], p_ref.at[0, 0], (xp, yp)),
                (lab_ref.at[CX], lab_ref.at[0], (xp, by)),
                (last_line_ref, line_ref, (bx, yp)),
            ]
        )
    ]

    def turned(n, carry):
        pair = lax.rem(n + CX // 2 - 1, CX // 2)
        load(pair).wait()
        for group in range(C // 16):
            block = jnp.concatenate(
                [
                    fbuf_ref[16 * group : 16 * group + 16, 2 * pair + half].reshape(256, CZ)
                    for half in range(2)
                ],
                axis=1,
            )
            out = jnp.dot(perm, block, preferred_element_type=jnp.float32).astype(jnp.bfloat16)
            for half in range(2):
                p_ref[1 + 2 * pair + half, 1 : CY + 1, 16 * group : 16 * group + 16, :] = out[
                    :, half * CZ : (half + 1) * CZ
                ].reshape(CY, 16, CZ)
        for copy in y_copies(pair):
            copy.start()
        return carry

    lax.fori_loop(0, 2, turned, 0)
    for copy in x_copies:
        copy.start()
    lax.fori_loop(2, CX // 2, turned, 0)

    def convolve(jobs, logit_ref):
        for pairs, sums_ref in zip(jobs, (sums_a, sums_b)):
            conv_dot(pairs, p_ref, w_ref, sums_ref)
        for pairs, sums_ref in zip(jobs, (sums_a, sums_b)):
            conv_head(pairs, sums_ref, bias_ref, head_ref, head_bias_ref, logit_ref)

    def early(n, carry):
        jobs = [
            [
                (1 + 4 * n + 2 * job + m, 4 * n + 2 * job + m, j)
                for m in range(2)
                for j in range(1, PAIRS - 1)
            ]
            for job in range(2)
        ]
        convolve(jobs, logit_a)
        return carry

    lax.fori_loop(0, EARLY // 4, early, 0)
    for copy in x_copies:
        copy.wait()
    for pair in range(CX // 2):
        for copy in y_copies(pair):
            copy.wait()

    @pl.when(bx == 0)
    def _():
        p_ref[0] = jnp.zeros((CY + 2, C, CZ), jnp.bfloat16)
        lab_ref[0] = jnp.full((CY, CZ), -1, jnp.int32)

    @pl.when(bx == NBX - 1)
    def _():
        p_ref[CX + 1] = jnp.zeros((CY + 2, C, CZ), jnp.bfloat16)

    @pl.when(by == 0)
    def _():
        p_ref[:, 0] = jnp.zeros((CX + 2, C, CZ), jnp.bfloat16)
        line_ref[...] = jnp.full((CX, CZ), -1, jnp.int32)

    @pl.when(by == NBY - 1)
    def _():
        p_ref[:, CY + 1] = jnp.zeros((CX + 2, C, CZ), jnp.bfloat16)

    jobs = [
        [(1 + 4 * job + m, 4 * job + m, j) for m in range(4) for j in (0, PAIRS - 1)]
        for job in range(2)
    ]
    convolve(jobs, logit_a)

    def plane(n, carry):
        late = [2 * n + m for m in range(2)]
        jobs = [[(lax.rem(k + EARLY + 1, CX), k, j) for j in range(PAIRS)] for k in late]
        for pairs, sums_ref in zip(jobs, (sums_a, sums_b)):
            conv_dot(pairs, p_ref, w_ref, sums_ref)
        found = []
        for k, pairs, sums_ref in zip(late, jobs, (sums_a, sums_b)):
            found.append(pair_sums(k + 1, k, logit_a, lab_ref, line_ref))
            conv_head(pairs, sums_ref, bias_ref, head_ref, head_bias_ref, logit_b)
        table_ref[...] += found[0] + found[1]
        return carry

    lax.fori_loop(0, (CX - EARLY) // 2, plane, 0)

    def late(n, carry):
        found = [
            pair_sums(lax.rem(k + EARLY + 1, CX), k, logit_b, lab_ref, line_ref)
            for k in (2 * n, 2 * n + 1)
        ]
        table_ref[...] += found[0] + found[1]
        return carry

    lax.fori_loop(0, (CX - EARLY) // 2, late, 0)
    rows = slot_rows(table_ref[...], ends_ref, owner_ref, row_ref, count_ref)
    for n in range(EO):
        rows_ref[n] = rows[n : n + 1, :]

    def give(peer_x, peer_y, slot):
        mine = rows_ref.at[peer_x * NBY + peer_y]
        remote(mine, got_ref.at[slot], row_send, row_recv, (peer_x, peer_y)).start()

    all_peers(give)
    others = pl.ds(1, DEVICES - 1)
    remote(
        rows_ref.at[others], got_ref.at[others], row_send, row_recv, (bx, lines[1])
    ).wait()
    totals = [rows_ref[me], got_ref[1], got_ref[2], got_ref[3]]
    for step in range(4, DEVICES):
        totals[step % 4] = totals[step % 4] + got_ref[step]
    total = (totals[0] + totals[1]) + (totals[2] + totals[3])
    o_ref[...] = total


def on_device(
    features,
    labels,
    conv_weight,
    conv_bias,
    head_weight,
    head_bias,
    edge_ends,
    edge_owner,
    edge_row,
    edge_count,
):
    bf16, f32, i32 = jnp.bfloat16, jnp.float32, jnp.int32
    total = pl.pallas_call(
        whole_kernel,
        out_shape=jax.ShapeDtypeStruct((1, EO), f32),
        in_specs=[pl.BlockSpec(memory_space=pl.ANY)] * 10,
        out_specs=VMEM,
        scratch_shapes=[
            pltpu.VMEM((C, 27 * C), bf16),
            pltpu.VMEM((1, C), f32),
            pltpu.VMEM((3, C), bf16),
            pltpu.SMEM((3,), f32),
            pltpu.VMEM((1, 2, SLOTS), i32),
            pltpu.VMEM((1, SLOTS), i32),
            pltpu.VMEM((1, SLOTS), i32),
            pltpu.VMEM((1, 1), i32),
            pltpu.VMEM((2 * C, CZ), f32),
            pltpu.VMEM((C, CX, CY, CZ), bf16),
            pltpu.VMEM((CX + 2, CY + 2, C, CZ), bf16),
            pltpu.VMEM((CX + 1, CY, CZ), i32),
            pltpu.VMEM((CX, CZ), i32),
            pltpu.VMEM((CX, CZ), i32),
            pltpu.VMEM((6 * C, 12 * C), bf16),
            pltpu.VMEM((EARLY, 3, CY, CZ), f32),
            pltpu.VMEM((CX - EARLY, 3, CY, CZ), f32),
            pltpu.VMEM((6 * C, 12 * CZ), f32),
            pltpu.VMEM((6 * C, 12 * CZ), f32),
            pltpu.VMEM((LABELS, LABELS), f32),
            pltpu.VMEM((DEVICES, 1, EO), f32),
            pltpu.VMEM((DEVICES, 1, EO), f32),
            pltpu.SemaphoreType.DMA((9,)),
            pltpu.SemaphoreType.DMA((CX // 2,)),
            pltpu.SemaphoreType.DMA((2, CX // 2)),
            pltpu.SemaphoreType.DMA((2, CX // 2)),
            pltpu.SemaphoreType.DMA((8,)),
            pltpu.SemaphoreType.DMA((8,)),
            pltpu.SemaphoreType.DMA,
            pltpu.SemaphoreType.DMA,
        ],
        compiler_params=pltpu.CompilerParams(
            collective_id=0, has_side_effects=True, vmem_limit_bytes=63 * 2**20
        ),
        name="whole",
    )(
        features,
        labels,
        conv_weight,
        conv_bias[None],
        head_weight,
        head_bias,
        edge_ends,
        edge_owner[:, :, 0],
        edge_row,
        edge_count[None],
    )
    return total[0]


def solution(mesh):
    placed = (
        P(None, "bx", "by", None),
        P("bx", "by", None),
        P(),
        P(),
        P(),
        P(),
        P(("bx", "by"), None, None),
        P(("bx", "by"), None, None),
        P(("bx", "by"), None),
        P(("bx", "by")),
    )
    return jax.shard_map(
        on_device, mesh=mesh, in_specs=placed, out_specs=P(("bx", "by")), check_vma=False
    )
```

```python
import jax
import jax.numpy as jnp
from jax import lax
from jax.experimental import pallas as pl
from jax.experimental.pallas import tpu as pltpu
from jax.sharding import PartitionSpec as P

LABELS = 256
EO = 128
NBX = 8
NBY = 16
CX = 16
CY = 16
CZ = 128
C = 64
SLOTS = 512
PAIRS = CY // 2
EARLY = 14
DEVICES = NBX * NBY
INNER_ROWS = tuple(range(2, CY - 2))
BORDER_ROWS = (0, 1, CY - 2, CY - 1)
MESH = pl.DeviceIdType.MESH
VMEM = pl.BlockSpec(memory_space=pltpu.VMEM)


def lay_weights(conv_ref, w_ref):
    blank = jnp.zeros((C, C), jnp.bfloat16)
    for dz in range(3):
        for out_y in range(2):
            pieces = []
            for dx in range(3):
                for in_y in range(4):
                    dy = in_y - out_y
                    at = (9 * dx + 3 * dy + dz) * C
                    pieces.append(conv_ref[:, at : at + C] if 0 <= dy <= 2 else blank)
            w_ref[(2 * dz + out_y) * C : (2 * dz + out_y + 1) * C, :] = jnp.concatenate(
                pieces, axis=1
            )


def conv_dot(pairs, p_ref, w_ref, sums_ref):
    stacked = jnp.concatenate(
        [
            jnp.concatenate(
                [p_ref[x + dx, 2 * j : 2 * j + 4].reshape(4 * C, CZ) for x, _, j in pairs], axis=1
            )
            for dx in range(3)
        ],
        axis=0,
    )
    sums_ref[:, : len(pairs) * CZ] = jnp.dot(
        w_ref[...], stacked, preferred_element_type=jnp.float32
    )


def conv_head(pairs, sums_ref, bias_ref, head_ref, head_bias_ref, logit_ref):
    lane = lax.broadcasted_iota(jnp.int32, (2 * C, CZ), 1)
    parts = []
    for n in range(len(pairs)):
        part = sums_ref[:, n * CZ : (n + 1) * CZ]
        before = pltpu.roll(part[: 2 * C], 1, 1)
        after = pltpu.roll(part[4 * C :], CZ - 1, 1)
        pre = (
            part[2 * C : 4 * C]
            + jnp.where(lane > 0, before, 0.0)
            + jnp.where(lane < CZ - 1, after, 0.0)
            + bias_ref[...]
        )
        parts.append(jnp.maximum(pre, 0.0).astype(jnp.bfloat16))
    hidden = jnp.concatenate([part[:C] for part in parts] + [part[C:] for part in parts], axis=1)
    logits = jnp.dot(head_ref[...], hidden, preferred_element_type=jnp.float32)
    for d in range(3):
        for n, (_, at, j) in enumerate(pairs):
            for out_y in range(2):
                col = (out_y * len(pairs) + n) * CZ
                y = 2 * j + out_y
                logit_ref[at, d, y : y + 1, :] = logits[d : d + 1, col : col + CZ] + head_bias_ref[d]


def pair_sums(x, at, logit_ref, lab_ref, line_ref, rows=tuple(range(CY))):
    affin = [
        jax.nn.sigmoid(logit_ref[at, d]).astype(jnp.bfloat16).astype(jnp.float32) for d in range(3)
    ]
    own_i = lab_ref[x + 1]
    line = lax.broadcasted_iota(jnp.int32, (CY, CZ), 0)
    deep = lax.broadcasted_iota(jnp.int32, (CY, CZ), 1)
    edge_line = own_i if line_ref is None else jnp.broadcast_to(line_ref[pl.ds(x, 1), :], (CY, CZ))
    own = own_i.astype(jnp.float32)
    oth_x = lab_ref[x].astype(jnp.float32)
    oth_y = jnp.where(line > 0, pltpu.roll(own_i, 1, 0), edge_line).astype(jnp.float32)
    oth_z = jnp.where(deep > 0, pltpu.roll(own_i, 1, 1), -1).astype(jnp.float32)
    same_xy = oth_x == oth_y
    same_xz = oth_x == oth_z
    same_yz = oth_y == oth_z
    sum_x = affin[0] + jnp.where(same_xy, affin[1], 0.0) + jnp.where(same_xz, affin[2], 0.0)
    sum_y = affin[1] + jnp.where(same_yz, affin[2], 0.0)
    top_x = sum_x.astype(jnp.bfloat16).astype(jnp.float32)
    top_y = sum_y.astype(jnp.bfloat16).astype(jnp.float32)
    in_x = same_xy | same_xz
    rest = jnp.where(in_x, sum_x - top_x, sum_y - top_y)
    rest_at = jnp.where(in_x, oth_x, oth_y)

    ids = lax.broadcasted_iota(jnp.int32, (LABELS, CZ), 0).astype(jnp.float32).astype(jnp.bfloat16)

    def spread_row(values, y):
        wide = jnp.broadcast_to(values[y : y + 1, :], (16, CZ)).astype(jnp.bfloat16)
        return jnp.concatenate([wide] * (LABELS // 16), axis=0)

    zero = jnp.zeros((LABELS, CZ), jnp.bfloat16)
    one = jnp.ones((LABELS, CZ), jnp.bfloat16)
    lefts, tops, rests = [], [], []
    for y in rows:
        lefts.append(jnp.where(spread_row(own, y) == ids, one, zero))
        tops.append(
            jnp.where(
                spread_row(oth_x, y) == ids,
                spread_row(top_x, y),
                jnp.where(
                    spread_row(oth_y, y) == ids,
                    spread_row(top_y, y),
                    jnp.where(spread_row(oth_z, y) == ids, spread_row(affin[2], y), zero),
                ),
            )
        )
        rests.append(jnp.where(spread_row(rest_at, y) == ids, spread_row(rest, y), zero))
    left = jnp.concatenate(lefts, axis=1)
    right = jnp.concatenate(
        [jnp.concatenate(tops, axis=1), jnp.concatenate(rests, axis=1)], axis=0
    )
    found = lax.dot_general(
        right, left, (((1,), (1,)), ((), ())), preferred_element_type=jnp.float32
    )
    return found[:LABELS] + found[LABELS:]


def two_terms(value, axis):
    top = value.astype(jnp.bfloat16)
    rest = (value - top.astype(jnp.float32)).astype(jnp.bfloat16)
    return jnp.concatenate([top, rest], axis=axis)


def one_hot(mask):
    return jnp.where(mask, 1.0, 0.0).astype(jnp.bfloat16)


def slot_rows(table, ends_ref, owner_ref, row_ref, count_ref):
    first = ends_ref[0, 0:1, :]
    second = ends_ref[0, 1:2, :]
    label = lax.broadcasted_iota(jnp.int32, (LABELS, SLOTS), 0)
    slot = lax.broadcasted_iota(jnp.int32, (1, SLOTS), 1)
    both = table + table.T
    picked = jnp.dot(
        two_terms(both, 0), one_hot(first == label), preferred_element_type=jnp.float32
    )
    picked = picked[:LABELS] + picked[LABELS:]
    value = jnp.sum(jnp.where(second == label, picked, 0.0), axis=0, keepdims=True)
    keep = (slot < count_ref[...]) & (first != second)
    value = jnp.where(keep, value, 0.0)
    row_id = lax.broadcasted_iota(jnp.int32, (EO, SLOTS), 0)
    spread = lax.dot_general(
        two_terms(jnp.where(owner_ref[...] == row_id, value, 0.0), 0),
        one_hot(row_ref[...] == row_id),
        (((1,), (1,)), ((), ())),
        preferred_element_type=jnp.float32,
    )
    return spread[:EO] + spread[EO:]


def whole_kernel(
    f_ref,
    own_hbm,
    conv_hbm,
    row_bias_hbm,
    head_hbm,
    head_bias_hbm,
    ends_hbm,
    owner_hbm,
    row_hbm,
    count_hbm,
    o_ref,
    conv_ref,
    row_bias_ref,
    head_ref,
    head_bias_ref,
    ends_ref,
    owner_ref,
    row_ref,
    count_ref,
    bias_ref,
    fbuf_ref,
    p_ref,
    lab_ref,
    line_ref,
    last_line_ref,
    w_ref,
    logit_a,
    logit_b,
    sums_a,
    sums_b,
    table_ref,
    rows_ref,
    got_ref,
    small_sem,
    load_sem,
    y_send,
    y_recv,
    x_send,
    x_recv,
    row_send,
    row_recv,
):
    bx = lax.axis_index("bx")
    by = lax.axis_index("by")
    xm = lax.rem(bx + NBX - 1, NBX)
    xp = lax.rem(bx + 1, NBX)
    ym = lax.rem(by + NBY - 1, NBY)
    yp = lax.rem(by + 1, NBY)
    me = bx * NBY + by
    barrier = pltpu.get_barrier_semaphore()

    lines = [lax.rem(by + step, NBY) for step in range(NBY)]

    def all_peers(visit):
        def one_x(step, carry):
            peer_x = lax.rem(bx + step, NBX)
            for n in range(NBY):
                visit(peer_x, lines[n], step * NBY + n)
            return carry

        for n in range(1, NBY):
            visit(bx, lines[n], n)
        lax.fori_loop(1, NBX, one_x, 0)

    def greet(peer_x, peer_y, slot):
        pl.semaphore_signal(barrier, inc=1, device_id=(peer_x, peer_y), device_id_type=MESH)

    def load(pair):
        at = pl.ds(2 * pair, 2)
        return pltpu.make_async_copy(f_ref.at[:, at], fbuf_ref.at[:, at], load_sem.at[pair])

    small = [
        pltpu.make_async_copy(src, dst, small_sem.at[n])
        for n, (src, dst) in enumerate(
            [
                (conv_hbm, conv_ref),
                (own_hbm, lab_ref.at[pl.ds(1, CX)]),
                (row_bias_hbm, row_bias_ref),
                (head_hbm, head_ref),
                (head_bias_hbm, head_bias_ref),
                (ends_hbm, ends_ref),
                (owner_hbm, owner_ref),
                (row_hbm, row_ref),
                (count_hbm, count_ref),
            ]
        )
    ]
    for copy in small:
        copy.start()
    for pair in (7, 0, 1, 2, 3, 4, 5, 6):
        load(pair).start()

    all_peers(greet)
    for copy in small:
        copy.wait()
    last_line_ref[...] = lab_ref[1:, CY - 1, :]
    diagonal = lax.broadcasted_iota(jnp.int32, (C, C), 0) == lax.broadcasted_iota(
        jnp.int32, (C, C), 1
    )
    column = jnp.sum(jnp.where(diagonal, row_bias_ref[...], 0.0), axis=1, keepdims=True)
    for out_y in range(2):
        bias_ref[out_y * C : (out_y + 1) * C, :] = jnp.broadcast_to(column, (C, CZ))
    lay_weights(conv_ref, w_ref)
    to = lax.broadcasted_iota(jnp.int32, (256, 256), 0)
    come = lax.broadcasted_iota(jnp.int32, (256, 256), 1)
    perm = ((to & 15) * 16 + (to >> 4) == come).astype(jnp.float32).astype(jnp.bfloat16)
    pl.semaphore_wait(barrier, DEVICES - 1)

    def remote(src, dst, send_sem, recv_sem, peer):
        return pltpu.make_async_remote_copy(
            src_ref=src,
            dst_ref=dst,
            send_sem=send_sem,
            recv_sem=recv_sem,
            device_id=peer,
            device_id_type=MESH,
        )

    def y_copies(pair):
        at = pl.ds(1 + 2 * pair, 2)
        return (
            remote(
                p_ref.at[at, 1], p_ref.at[at, CY + 1], y_send.at[0, pair], y_recv.at[0, pair], (bx, ym)
            ),
            remote(
                p_ref.at[at, CY], p_ref.at[at, 0], y_send.at[1, pair], y_recv.at[1, pair], (bx, yp)
            ),
        )

    inner = pl.ds(1, CY)
    x_copies = [
        remote(src, dst, x_send.at[n], x_recv.at[n], peer)
        for n, (src, dst, peer) in enumerate(
            [
                (p_ref.at[1, inner], p_ref.at[CX + 1, inner], (xm, by)),
                (p_ref.at[1, 1], p_ref.at[CX + 1, CY + 1], (xm, ym)),
                (p_ref.at[1, CY], p_ref.at[CX + 1, 0], (xm, yp)),
                (p_ref.at[CX, inner], p_ref.at[0, inner], (xp, by)),
                (p_ref.at[CX, 1], p_ref.at[0, CY + 1], (xp, ym)),
                (p_ref.at[CX, CY], p_ref.at[0, 0], (xp, yp)),
                (lab_ref.at[CX], lab_ref.at[0], (xp, by)),
                (last_line_ref, line_ref, (bx, yp)),
            ]
        )
    ]

    def turned(n, carry):
        pair = lax.rem(n + CX // 2 - 1, CX // 2)
        load(pair).wait()
        for group in range(C // 16):
            block = jnp.concatenate(
                [
                    fbuf_ref[16 * group : 16 * group + 16, 2 * pair + half].reshape(256, CZ)
                    for half in range(2)
                ],
                axis=1,
            )
            out = jnp.dot(perm, block, preferred_element_type=jnp.float32).astype(jnp.bfloat16)
            for half in range(2):
                p_ref[1 + 2 * pair + half, 1 : CY + 1, 16 * group : 16 * group + 16, :] = out[
                    :, half * CZ : (half + 1) * CZ
                ].reshape(CY, 16, CZ)
        for copy in y_copies(pair):
            copy.start()
        return carry

    lax.fori_loop(0, 2, turned, 0)
    for copy in x_copies:
        copy.start()
    lax.fori_loop(2, CX // 2, turned, 0)

    def convolve(jobs, logit_ref):
        for pairs, sums_ref in zip(jobs, (sums_a, sums_b)):
            conv_dot(pairs, p_ref, w_ref, sums_ref)
        for pairs, sums_ref in zip(jobs, (sums_a, sums_b)):
            conv_head(pairs, sums_ref, bias_ref, head_ref, head_bias_ref, logit_ref)

    def inner_pairs(at):
        return [(1 + at + m, at + m, j) for m in range(2) for j in range(1, PAIRS - 1)]

    def early(n, carry):
        convolve([inner_pairs(4 * n), inner_pairs(4 * n + 2)], logit_a)
        return carry

    lax.fori_loop(0, (EARLY - 2) // 4, early, 0)
    conv_dot(inner_pairs(EARLY - 2), p_ref, w_ref, sums_a)
    found = [
        pair_sums(at + 1, at, logit_a, lab_ref, None, INNER_ROWS) for at in range(2)
    ]
    conv_head(inner_pairs(EARLY - 2), sums_a, bias_ref, head_ref, head_bias_ref, logit_a)
    table_ref[...] = found[0] + found[1]
    for copy in x_copies:
        copy.wait()
    for pair in range(CX // 2):
        for copy in y_copies(pair):
            copy.wait()

    @pl.when(bx == 0)
    def _():
        p_ref[0] = jnp.zeros((CY + 2, C, CZ), jnp.bfloat16)
        lab_ref[0] = jnp.full((CY, CZ), -1, jnp.int32)

    @pl.when(bx == NBX - 1)
    def _():
        p_ref[CX + 1] = jnp.zeros((CY + 2, C, CZ), jnp.bfloat16)

    @pl.when(by == 0)
    def _():
        p_ref[:, 0] = jnp.zeros((CX + 2, C, CZ), jnp.bfloat16)
        line_ref[...] = jnp.full((CX, CZ), -1, jnp.int32)

    @pl.when(by == NBY - 1)
    def _():
        p_ref[:, CY + 1] = jnp.zeros((CX + 2, C, CZ), jnp.bfloat16)

    half = EARLY // 2
    jobs = [
        [(1 + half * job + m, half * job + m, j) for m in range(half) for j in (0, PAIRS - 1)]
        for job in range(2)
    ]
    convolve(jobs, logit_a)

    ends = (CX - 1, 0)
    jobs = [[(x, k, j) for j in range(PAIRS)] for k, x in enumerate(ends)]
    for pairs, sums_ref in zip(jobs, (sums_a, sums_b)):
        conv_dot(pairs, p_ref, w_ref, sums_ref)
    found = []
    for at, pairs, sums_ref in zip((2, 3), jobs, (sums_a, sums_b)):
        found.append(pair_sums(at + 1, at, logit_a, lab_ref, line_ref))
        conv_head(pairs, sums_ref, bias_ref, head_ref, head_bias_ref, logit_b)
    table_ref[...] += found[0] + found[1]

    def late(n, carry):
        found = [pair_sums(k + 1, k, logit_a, lab_ref, line_ref) for k in (2 * n, 2 * n + 1)]
        table_ref[...] += found[0] + found[1]
        return carry

    lax.fori_loop(2, EARLY // 2, late, 0)
    found = [pair_sums(x, k, logit_b, lab_ref, line_ref) for k, x in enumerate(ends)]
    found += [pair_sums(at + 1, at, logit_a, lab_ref, line_ref, BORDER_ROWS) for at in range(2)]
    table_ref[...] += (found[0] + found[1]) + (found[2] + found[3])
    rows = slot_rows(table_ref[...], ends_ref, owner_ref, row_ref, count_ref)
    for n in range(EO):
        rows_ref[n] = rows[n : n + 1, :]

    def give(peer_x, peer_y, slot):
        mine = rows_ref.at[peer_x * NBY + peer_y]
        remote(mine, got_ref.at[slot], row_send, row_recv, (peer_x, peer_y)).start()

    all_peers(give)
    others = pl.ds(1, DEVICES - 1)
    remote(
        rows_ref.at[others], got_ref.at[others], row_send, row_recv, (bx, lines[1])
    ).wait()
    totals = [rows_ref[me], got_ref[1], got_ref[2], got_ref[3]]
    for step in range(4, DEVICES):
        totals[step % 4] = totals[step % 4] + got_ref[step]
    total = (totals[0] + totals[1]) + (totals[2] + totals[3])
    o_ref[...] = total


def on_device(
    features,
    labels,
    conv_weight,
    conv_bias,
    head_weight,
    head_bias,
    edge_ends,
    edge_owner,
    edge_row,
    edge_count,
):
    bf16, f32, i32 = jnp.bfloat16, jnp.float32, jnp.int32
    total = pl.pallas_call(
        whole_kernel,
        out_shape=jax.ShapeDtypeStruct((1, EO), f32),
        in_specs=[pl.BlockSpec(memory_space=pl.ANY)] * 10,
        out_specs=VMEM,
        scratch_shapes=[
            pltpu.VMEM((C, 27 * C), bf16),
            pltpu.VMEM((1, C), f32),
            pltpu.VMEM((3, C), bf16),
            pltpu.SMEM((3,), f32),
            pltpu.VMEM((1, 2, SLOTS), i32),
            pltpu.VMEM((1, SLOTS), i32),
            pltpu.VMEM((1, SLOTS), i32),
            pltpu.VMEM((1, 1), i32),
            pltpu.VMEM((2 * C, CZ), f32),
            pltpu.VMEM((C, CX, CY, CZ), bf16),
            pltpu.VMEM((CX + 2, CY + 2, C, CZ), bf16),
            pltpu.VMEM((CX + 1, CY, CZ), i32),
            pltpu.VMEM((CX, CZ), i32),
            pltpu.VMEM((CX, CZ), i32),
            pltpu.VMEM((6 * C, 12 * C), bf16),
            pltpu.VMEM((EARLY, 3, CY, CZ), f32),
            pltpu.VMEM((CX - EARLY, 3, CY, CZ), f32),
            pltpu.VMEM((6 * C, EARLY * CZ), f32),
            pltpu.VMEM((6 * C, EARLY * CZ), f32),
            pltpu.VMEM((LABELS, LABELS), f32),
            pltpu.VMEM((DEVICES, 1, EO), f32),
            pltpu.VMEM((DEVICES, 1, EO), f32),
            pltpu.SemaphoreType.DMA((9,)),
            pltpu.SemaphoreType.DMA((CX // 2,)),
            pltpu.SemaphoreType.DMA((2, CX // 2)),
            pltpu.SemaphoreType.DMA((2, CX // 2)),
            pltpu.SemaphoreType.DMA((8,)),
            pltpu.SemaphoreType.DMA((8,)),
            pltpu.SemaphoreType.DMA,
            pltpu.SemaphoreType.DMA,
        ],
        compiler_params=pltpu.CompilerParams(
            collective_id=0, has_side_effects=True, vmem_limit_bytes=63 * 2**20
        ),
        name="whole",
    )(
        features,
        labels,
        conv_weight,
        conv_bias[None],
        head_weight,
        head_bias,
        edge_ends,
        edge_owner[:, :, 0],
        edge_row,
        edge_count[None],
    )
    return total[0]


def solution(mesh):
    placed = (
        P(None, "bx", "by", None),
        P("bx", "by", None),
        P(),
        P(),
        P(),
        P(),
        P(("bx", "by"), None, None),
        P(("bx", "by"), None, None),
        P(("bx", "by"), None),
        P(("bx", "by")),
    )
    return jax.shard_map(
        on_device, mesh=mesh, in_specs=placed, out_specs=P(("bx", "by")), check_vma=False
    )
```

```python
import functools

import jax
import jax.numpy as jnp
from jax import lax
from jax.experimental import pallas as pl
from jax.experimental.pallas import tpu as pltpu
from jax.sharding import PartitionSpec as P

LABELS = 256
EO = 128
NBX = 8
NBY = 16
CX = 16
CY = 16
CZ = 128
C = 64
SLOTS = 512
PAIRS = CY // 2
EARLY = 14
INNER = 6
DEVICES = NBX * NBY
INNER_ROWS = tuple(range(2, CY - 2))
BORDER_ROWS = (0, 1, CY - 2, CY - 1)
MESH = pl.DeviceIdType.MESH
VMEM = pl.BlockSpec(memory_space=pltpu.VMEM)


def lay_weights(conv_ref, w_ref):
    blank = jnp.zeros((C, C), jnp.bfloat16)
    for dz in range(3):
        for out_y in range(2):
            pieces = []
            for dx in range(3):
                for in_y in range(4):
                    dy = in_y - out_y
                    at = (9 * dx + 3 * dy + dz) * C
                    pieces.append(conv_ref[:, at : at + C] if 0 <= dy <= 2 else blank)
            w_ref[(2 * dz + out_y) * C : (2 * dz + out_y + 1) * C, :] = jnp.concatenate(
                pieces, axis=1
            )


def conv_dot(pairs, p_ref, w_ref, sums_ref):
    stacked = jnp.concatenate(
        [
            jnp.concatenate(
                [p_ref[x + dx, 2 * j : 2 * j + 4].reshape(4 * C, CZ) for x, _, j in pairs], axis=1
            )
            for dx in range(3)
        ],
        axis=0,
    )
    sums_ref[:, : len(pairs) * CZ] = jnp.dot(
        w_ref[...], stacked, preferred_element_type=jnp.float32
    )


def conv_head(pairs, sums_ref, bias_ref, head_ref, head_bias_ref, logit_ref):
    lane = lax.broadcasted_iota(jnp.int32, (2 * C, CZ), 1)
    parts = []
    for n in range(len(pairs)):
        part = sums_ref[:, n * CZ : (n + 1) * CZ]
        before = pltpu.roll(part[: 2 * C], 1, 1)
        after = pltpu.roll(part[4 * C :], CZ - 1, 1)
        pre = (
            part[2 * C : 4 * C]
            + jnp.where(lane > 0, before, 0.0)
            + jnp.where(lane < CZ - 1, after, 0.0)
            + bias_ref[...]
        )
        parts.append(jnp.maximum(pre, 0.0).astype(jnp.bfloat16))
    hidden = jnp.concatenate([part[:C] for part in parts] + [part[C:] for part in parts], axis=1)
    logits = jnp.dot(head_ref[...], hidden, preferred_element_type=jnp.float32)
    for d in range(3):
        for n, (_, at, j) in enumerate(pairs):
            for out_y in range(2):
                col = (out_y * len(pairs) + n) * CZ
                y = 2 * j + out_y
                logit_ref[at, d, y : y + 1, :] = logits[d : d + 1, col : col + CZ] + head_bias_ref[d]


def pair_sums(x, at, logit_ref, lab_ref, line_ref, rows=tuple(range(CY))):
    affin = [
        jax.nn.sigmoid(logit_ref[at, d]).astype(jnp.bfloat16).astype(jnp.float32) for d in range(3)
    ]
    own_i = lab_ref[x + 1]
    line = lax.broadcasted_iota(jnp.int32, (CY, CZ), 0)
    deep = lax.broadcasted_iota(jnp.int32, (CY, CZ), 1)
    edge_line = own_i if line_ref is None else jnp.broadcast_to(line_ref[pl.ds(x, 1), :], (CY, CZ))
    own = own_i.astype(jnp.float32)
    oth_x = lab_ref[x].astype(jnp.float32)
    oth_y = jnp.where(line > 0, pltpu.roll(own_i, 1, 0), edge_line).astype(jnp.float32)
    oth_z = jnp.where(deep > 0, pltpu.roll(own_i, 1, 1), -1).astype(jnp.float32)
    same_xy = oth_x == oth_y
    same_xz = oth_x == oth_z
    same_yz = oth_y == oth_z
    sum_x = affin[0] + jnp.where(same_xy, affin[1], 0.0) + jnp.where(same_xz, affin[2], 0.0)
    sum_y = affin[1] + jnp.where(same_yz, affin[2], 0.0)
    top_x = sum_x.astype(jnp.bfloat16).astype(jnp.float32)
    top_y = sum_y.astype(jnp.bfloat16).astype(jnp.float32)
    in_x = same_xy | same_xz
    rest = jnp.where(in_x, sum_x - top_x, sum_y - top_y)
    rest_at = jnp.where(in_x, oth_x, oth_y)

    ids = lax.broadcasted_iota(jnp.int32, (LABELS, CZ), 0).astype(jnp.float32).astype(jnp.bfloat16)

    def spread_row(values, y):
        wide = jnp.broadcast_to(values[y : y + 1, :], (16, CZ)).astype(jnp.bfloat16)
        return jnp.concatenate([wide] * (LABELS // 16), axis=0)

    zero = jnp.zeros((LABELS, CZ), jnp.bfloat16)
    one = jnp.ones((LABELS, CZ), jnp.bfloat16)
    lefts, tops, rests = [], [], []
    for y in rows:
        lefts.append(jnp.where(spread_row(own, y) == ids, one, zero))
        tops.append(
            jnp.where(
                spread_row(oth_x, y) == ids,
                spread_row(top_x, y),
                jnp.where(
                    spread_row(oth_y, y) == ids,
                    spread_row(top_y, y),
                    jnp.where(spread_row(oth_z, y) == ids, spread_row(affin[2], y), zero),
                ),
            )
        )
        rests.append(jnp.where(spread_row(rest_at, y) == ids, spread_row(rest, y), zero))
    left = jnp.concatenate(lefts, axis=1)
    right = jnp.concatenate(
        [jnp.concatenate(tops, axis=1), jnp.concatenate(rests, axis=1)], axis=0
    )
    found = lax.dot_general(
        right, left, (((1,), (1,)), ((), ())), preferred_element_type=jnp.float32
    )
    return found[:LABELS] + found[LABELS:]


def two_terms(value, axis):
    top = value.astype(jnp.bfloat16)
    rest = (value - top.astype(jnp.float32)).astype(jnp.bfloat16)
    return jnp.concatenate([top, rest], axis=axis)


def one_hot(mask):
    return jnp.where(mask, 1.0, 0.0).astype(jnp.bfloat16)


def slot_rows(table, ends_ref, owner_ref, row_ref, count_ref):
    first = ends_ref[0, 0:1, :]
    second = ends_ref[0, 1:2, :]
    label = lax.broadcasted_iota(jnp.int32, (LABELS, SLOTS), 0)
    slot = lax.broadcasted_iota(jnp.int32, (1, SLOTS), 1)
    both = table + table.T
    picked = jnp.dot(
        two_terms(both, 0), one_hot(first == label), preferred_element_type=jnp.float32
    )
    picked = picked[:LABELS] + picked[LABELS:]
    value = jnp.sum(jnp.where(second == label, picked, 0.0), axis=0, keepdims=True)
    keep = (slot < count_ref[...]) & (first != second)
    value = jnp.where(keep, value, 0.0)
    row_id = lax.broadcasted_iota(jnp.int32, (EO, SLOTS), 0)
    spread = lax.dot_general(
        two_terms(jnp.where(owner_ref[...] == row_id, value, 0.0), 0),
        one_hot(row_ref[...] == row_id),
        (((1,), (1,)), ((), ())),
        preferred_element_type=jnp.float32,
    )
    return spread[:EO] + spread[EO:]


def whole_kernel(
    f_ref,
    own_hbm,
    conv_hbm,
    row_bias_hbm,
    head_hbm,
    head_bias_hbm,
    ends_hbm,
    owner_hbm,
    row_hbm,
    count_hbm,
    o_ref,
    conv_ref,
    row_bias_ref,
    head_ref,
    head_bias_ref,
    ends_ref,
    owner_ref,
    row_ref,
    count_ref,
    bias_ref,
    fbuf_ref,
    p_ref,
    lab_ref,
    line_ref,
    last_line_ref,
    w_ref,
    logit_a,
    logit_b,
    sums_a,
    sums_b,
    table_ref,
    rows_ref,
    got_ref,
    small_sem,
    load_sem,
    y_send,
    y_recv,
    x_send,
    x_recv,
    row_send,
    row_recv,
):
    bx = lax.axis_index("bx")
    by = lax.axis_index("by")
    xm = lax.rem(bx + NBX - 1, NBX)
    xp = lax.rem(bx + 1, NBX)
    ym = lax.rem(by + NBY - 1, NBY)
    yp = lax.rem(by + 1, NBY)
    me = bx * NBY + by
    barrier = pltpu.get_barrier_semaphore()

    lines = [lax.rem(by + step, NBY) for step in range(NBY)]

    def all_peers(visit):
        def one_x(step, carry):
            peer_x = lax.rem(bx + step, NBX)
            for n in range(NBY):
                visit(peer_x, lines[n], step * NBY + n)
            return carry

        for n in range(1, NBY):
            visit(bx, lines[n], n)
        lax.fori_loop(1, NBX, one_x, 0)

    def greet(peer_x, peer_y, slot):
        pl.semaphore_signal(barrier, inc=1, device_id=(peer_x, peer_y), device_id_type=MESH)

    def load(pair):
        at = pl.ds(2 * pair, 2)
        return pltpu.make_async_copy(f_ref.at[:, at], fbuf_ref.at[:, at], load_sem.at[pair])

    small = [
        pltpu.make_async_copy(src, dst, small_sem.at[n])
        for n, (src, dst) in enumerate(
            [
                (conv_hbm, conv_ref),
                (own_hbm, lab_ref.at[pl.ds(1, CX)]),
                (row_bias_hbm, row_bias_ref),
                (head_hbm, head_ref),
                (head_bias_hbm, head_bias_ref),
                (ends_hbm, ends_ref),
                (owner_hbm, owner_ref),
                (row_hbm, row_ref),
                (count_hbm, count_ref),
            ]
        )
    ]
    for copy in small:
        copy.start()
    for pair in (7, 0, 1, 2, 3, 4, 5, 6):
        load(pair).start()

    all_peers(greet)
    for copy in small:
        copy.wait()
    last_line_ref[...] = lab_ref[1:, CY - 1, :]
    diagonal = lax.broadcasted_iota(jnp.int32, (C, C), 0) == lax.broadcasted_iota(
        jnp.int32, (C, C), 1
    )
    column = jnp.sum(jnp.where(diagonal, row_bias_ref[...], 0.0), axis=1, keepdims=True)
    for out_y in range(2):
        bias_ref[out_y * C : (out_y + 1) * C, :] = jnp.broadcast_to(column, (C, CZ))
    lay_weights(conv_ref, w_ref)
    to = lax.broadcasted_iota(jnp.int32, (256, 256), 0)
    come = lax.broadcasted_iota(jnp.int32, (256, 256), 1)
    perm = ((to & 15) * 16 + (to >> 4) == come).astype(jnp.float32).astype(jnp.bfloat16)
    pl.semaphore_wait(barrier, DEVICES - 1)

    def remote(src, dst, send_sem, recv_sem, peer):
        return pltpu.make_async_remote_copy(
            src_ref=src,
            dst_ref=dst,
            send_sem=send_sem,
            recv_sem=recv_sem,
            device_id=peer,
            device_id_type=MESH,
        )

    def y_copies(pair):
        at = pl.ds(1 + 2 * pair, 2)
        return (
            remote(
                p_ref.at[at, 1], p_ref.at[at, CY + 1], y_send.at[0, pair], y_recv.at[0, pair], (bx, ym)
            ),
            remote(
                p_ref.at[at, CY], p_ref.at[at, 0], y_send.at[1, pair], y_recv.at[1, pair], (bx, yp)
            ),
        )

    inner = pl.ds(1, CY)
    x_copies = [
        remote(src, dst, x_send.at[n], x_recv.at[n], peer)
        for n, (src, dst, peer) in enumerate(
            [
                (p_ref.at[1, inner], p_ref.at[CX + 1, inner], (xm, by)),
                (p_ref.at[1, 1], p_ref.at[CX + 1, CY + 1], (xm, ym)),
                (p_ref.at[1, CY], p_ref.at[CX + 1, 0], (xm, yp)),
                (p_ref.at[CX, inner], p_ref.at[0, inner], (xp, by)),
                (p_ref.at[CX, 1], p_ref.at[0, CY + 1], (xp, ym)),
                (p_ref.at[CX, CY], p_ref.at[0, 0], (xp, yp)),
                (lab_ref.at[CX], lab_ref.at[0], (xp, by)),
                (last_line_ref, line_ref, (bx, yp)),
            ]
        )
    ]

    def turn(pair):
        for group in range(C // 16):
            block = jnp.concatenate(
                [
                    fbuf_ref[16 * group : 16 * group + 16, 2 * pair + half].reshape(256, CZ)
                    for half in range(2)
                ],
                axis=1,
            )
            out = jnp.dot(perm, block, preferred_element_type=jnp.float32).astype(jnp.bfloat16)
            for half in range(2):
                p_ref[1 + 2 * pair + half, 1 : CY + 1, 16 * group : 16 * group + 16, :] = out[
                    :, half * CZ : (half + 1) * CZ
                ].reshape(CY, 16, CZ)

    def turned(n, carry):
        pair = lax.rem(n + CX // 2 - 1, CX // 2)
        load(pair).wait()
        turn(pair)
        for copy in y_copies(pair):
            copy.start()
        return carry

    lax.fori_loop(0, 2, turned, 0)
    for copy in x_copies:
        copy.start()
    lax.fori_loop(2, 3, turned, 0)

    def convolve(jobs, logit_ref):
        for pairs, sums_ref in zip(jobs, (sums_a, sums_b)):
            conv_dot(pairs, p_ref, w_ref, sums_ref)
        for pairs, sums_ref in zip(jobs, (sums_a, sums_b)):
            conv_head(pairs, sums_ref, bias_ref, head_ref, head_bias_ref, logit_ref)

    def inner_pairs(at):
        return [(1 + at + m, at + m, j) for m in range(2) for j in range(1, PAIRS - 1)]

    def early(n, carry):
        load(n + 2).wait()
        conv_dot(inner_pairs(2 * n), p_ref, w_ref, sums_a)
        turn(n + 2)
        conv_head(inner_pairs(2 * n), sums_a, bias_ref, head_ref, head_bias_ref, logit_a)
        for copy in y_copies(n + 2):
            copy.start()
        return carry

    lax.fori_loop(0, CX // 2 - 3, early, 0)
    jobs = (inner_pairs(EARLY - 4), inner_pairs(EARLY - 2))
    for pairs, sums_ref in zip(jobs, (sums_a, sums_b)):
        conv_dot(pairs, p_ref, w_ref, sums_ref)
    found = []
    for at, pairs, sums_ref in zip(range(2), jobs, (sums_a, sums_b)):
        found.append(pair_sums(at + 1, at, logit_a, lab_ref, None, INNER_ROWS))
        conv_head(pairs, sums_ref, bias_ref, head_ref, head_bias_ref, logit_a)
    table_ref[...] = found[0] + found[1]

    def inner_sums(n, carry):
        found = [
            pair_sums(at + 1, at, logit_a, lab_ref, None, INNER_ROWS) for at in (2 * n, 2 * n + 1)
        ]
        table_ref[...] += found[0] + found[1]
        return carry

    lax.fori_loop(1, INNER // 2, inner_sums, 0)
    for copy in x_copies:
        copy.wait()
    for pair in range(CX // 2):
        for copy in y_copies(pair):
            copy.wait()

    @pl.when(bx == 0)
    def _():
        p_ref[0] = jnp.zeros((CY + 2, C, CZ), jnp.bfloat16)
        lab_ref[0] = jnp.full((CY, CZ), -1, jnp.int32)

    @pl.when(bx == NBX - 1)
    def _():
        p_ref[CX + 1] = jnp.zeros((CY + 2, C, CZ), jnp.bfloat16)

    @pl.when(by == 0)
    def _():
        p_ref[:, 0] = jnp.zeros((CX + 2, C, CZ), jnp.bfloat16)
        line_ref[...] = jnp.full((CX, CZ), -1, jnp.int32)

    @pl.when(by == NBY - 1)
    def _():
        p_ref[:, CY + 1] = jnp.zeros((CX + 2, C, CZ), jnp.bfloat16)

    half = EARLY // 2

    def border(job, carry):
        at = half * job
        pairs = [(1 + at + m, at + m, j) for m in range(half) for j in (0, PAIRS - 1)]
        conv_dot(pairs, p_ref, w_ref, sums_a)
        conv_head(pairs, sums_a, bias_ref, head_ref, head_bias_ref, logit_a)
        return carry

    lax.fori_loop(0, 2, border, 0)

    ends = (CX - 1, 0)
    jobs = [[(x, k, j) for j in range(PAIRS)] for k, x in enumerate(ends)]
    for pairs, sums_ref in zip(jobs, (sums_a, sums_b)):
        conv_dot(pairs, p_ref, w_ref, sums_ref)
    found = []
    for at, pairs, sums_ref in zip((INNER, INNER + 1), jobs, (sums_a, sums_b)):
        found.append(pair_sums(at + 1, at, logit_a, lab_ref, line_ref))
        conv_head(pairs, sums_ref, bias_ref, head_ref, head_bias_ref, logit_b)
    table_ref[...] += found[0] + found[1]

    def late(n, carry):
        found = [pair_sums(k + 1, k, logit_a, lab_ref, line_ref) for k in (2 * n, 2 * n + 1)]
        table_ref[...] += found[0] + found[1]
        return carry

    lax.fori_loop(INNER // 2 + 1, EARLY // 2, late, 0)
    found = [pair_sums(x, k, logit_b, lab_ref, line_ref) for k, x in enumerate(ends)]
    found += [pair_sums(at + 1, at, logit_a, lab_ref, line_ref, BORDER_ROWS) for at in range(INNER)]
    table_ref[...] += functools.reduce(jnp.add, found)
    rows = slot_rows(table_ref[...], ends_ref, owner_ref, row_ref, count_ref)
    for n in range(EO):
        rows_ref[n] = rows[n : n + 1, :]

    def give(peer_x, peer_y, slot):
        mine = rows_ref.at[peer_x * NBY + peer_y]
        remote(mine, got_ref.at[slot], row_send, row_recv, (peer_x, peer_y)).start()

    all_peers(give)
    others = pl.ds(1, DEVICES - 1)
    remote(
        rows_ref.at[others], got_ref.at[others], row_send, row_recv, (bx, lines[1])
    ).wait()
    totals = [rows_ref[me], got_ref[1], got_ref[2], got_ref[3]]
    for step in range(4, DEVICES):
        totals[step % 4] = totals[step % 4] + got_ref[step]
    total = (totals[0] + totals[1]) + (totals[2] + totals[3])
    o_ref[...] = total


def on_device(
    features,
    labels,
    conv_weight,
    conv_bias,
    head_weight,
    head_bias,
    edge_ends,
    edge_owner,
    edge_row,
    edge_count,
):
    bf16, f32, i32 = jnp.bfloat16, jnp.float32, jnp.int32
    total = pl.pallas_call(
        whole_kernel,
        out_shape=jax.ShapeDtypeStruct((1, EO), f32),
        in_specs=[pl.BlockSpec(memory_space=pl.ANY)] * 10,
        out_specs=VMEM,
        scratch_shapes=[
            pltpu.VMEM((C, 27 * C), bf16),
            pltpu.VMEM((1, C), f32),
            pltpu.VMEM((3, C), bf16),
            pltpu.SMEM((3,), f32),
            pltpu.VMEM((1, 2, SLOTS), i32),
            pltpu.VMEM((1, SLOTS), i32),
            pltpu.VMEM((1, SLOTS), i32),
            pltpu.VMEM((1, 1), i32),
            pltpu.VMEM((2 * C, CZ), f32),
            pltpu.VMEM((C, CX, CY, CZ), bf16),
            pltpu.VMEM((CX + 2, CY + 2, C, CZ), bf16),
            pltpu.VMEM((CX + 1, CY, CZ), i32),
            pltpu.VMEM((CX, CZ), i32),
            pltpu.VMEM((CX, CZ), i32),
            pltpu.VMEM((6 * C, 12 * C), bf16),
            pltpu.VMEM((EARLY, 3, CY, CZ), f32),
            pltpu.VMEM((CX - EARLY, 3, CY, CZ), f32),
            pltpu.VMEM((6 * C, EARLY * CZ), f32),
            pltpu.VMEM((6 * C, EARLY * CZ), f32),
            pltpu.VMEM((LABELS, LABELS), f32),
            pltpu.VMEM((DEVICES, 1, EO), f32),
            pltpu.VMEM((DEVICES, 1, EO), f32),
            pltpu.SemaphoreType.DMA((9,)),
            pltpu.SemaphoreType.DMA((CX // 2,)),
            pltpu.SemaphoreType.DMA((2, CX // 2)),
            pltpu.SemaphoreType.DMA((2, CX // 2)),
            pltpu.SemaphoreType.DMA((8,)),
            pltpu.SemaphoreType.DMA((8,)),
            pltpu.SemaphoreType.DMA,
            pltpu.SemaphoreType.DMA,
        ],
        compiler_params=pltpu.CompilerParams(
            collective_id=0, has_side_effects=True, vmem_limit_bytes=63 * 2**20
        ),
        name="whole",
    )(
        features,
        labels,
        conv_weight,
        conv_bias[None],
        head_weight,
        head_bias,
        edge_ends,
        edge_owner[:, :, 0],
        edge_row,
        edge_count[None],
    )
    return total[0]


def solution(mesh):
    placed = (
        P(None, "bx", "by", None),
        P("bx", "by", None),
        P(),
        P(),
        P(),
        P(),
        P(("bx", "by"), None, None),
        P(("bx", "by"), None, None),
        P(("bx", "by"), None),
        P(("bx", "by")),
    )
    return jax.shard_map(
        on_device, mesh=mesh, in_specs=placed, out_specs=P(("bx", "by")), check_vma=False
    )
```

```python
import functools

import jax
import jax.numpy as jnp
from jax import lax
from jax.experimental import pallas as pl
from jax.experimental.pallas import tpu as pltpu
from jax.sharding import PartitionSpec as P

LABELS = 256
EO = 128
NBX = 8
NBY = 16
CX = 16
CY = 16
CZ = 128
C = 64
SLOTS = 512
PAIRS = CY // 2
EARLY = 14
INNER = 6
DEVICES = NBX * NBY
INNER_ROWS = tuple(range(2, CY - 2))
BORDER_ROWS = (0, 1, CY - 2, CY - 1)
MESH = pl.DeviceIdType.MESH
VMEM = pl.BlockSpec(memory_space=pltpu.VMEM)


def lay_weights(conv_ref, w_ref):
    blank = jnp.zeros((C, C), jnp.bfloat16)
    for dz in range(3):
        for out_y in range(2):
            pieces = []
            for dx in range(3):
                for in_y in range(4):
                    dy = in_y - out_y
                    at = (9 * dx + 3 * dy + dz) * C
                    pieces.append(conv_ref[:, at : at + C] if 0 <= dy <= 2 else blank)
            w_ref[(2 * dz + out_y) * C : (2 * dz + out_y + 1) * C, :] = jnp.concatenate(
                pieces, axis=1
            )


def conv_dot(pairs, p_ref, w_ref, sums_ref):
    stacked = jnp.concatenate(
        [
            jnp.concatenate(
                [p_ref[x + dx, 2 * j : 2 * j + 4].reshape(4 * C, CZ) for x, _, j in pairs], axis=1
            )
            for dx in range(3)
        ],
        axis=0,
    )
    sums_ref[:, : len(pairs) * CZ] = jnp.dot(
        w_ref[...], stacked, preferred_element_type=jnp.float32
    )


def conv_head(pairs, sums_ref, bias_ref, head_ref, head_bias_ref, logit_ref):
    lane = lax.broadcasted_iota(jnp.int32, (2 * C, CZ), 1)
    parts = []
    for n in range(len(pairs)):
        part = sums_ref[:, n * CZ : (n + 1) * CZ]
        before = pltpu.roll(part[: 2 * C], 1, 1)
        after = pltpu.roll(part[4 * C :], CZ - 1, 1)
        pre = (
            part[2 * C : 4 * C]
            + jnp.where(lane > 0, before, 0.0)
            + jnp.where(lane < CZ - 1, after, 0.0)
            + bias_ref[...]
        )
        parts.append(jnp.maximum(pre, 0.0).astype(jnp.bfloat16))
    hidden = jnp.concatenate([part[:C] for part in parts] + [part[C:] for part in parts], axis=1)
    logits = jnp.dot(head_ref[...], hidden, preferred_element_type=jnp.float32)
    for d in range(3):
        for n, (_, at, j) in enumerate(pairs):
            for out_y in range(2):
                col = (out_y * len(pairs) + n) * CZ
                y = 2 * j + out_y
                logit_ref[at, d, y : y + 1, :] = logits[d : d + 1, col : col + CZ] + head_bias_ref[d]


def pair_sums(x, at, logit_ref, lab_ref, line_ref, rows=tuple(range(CY))):
    affin = [
        jax.nn.sigmoid(logit_ref[at, d]).astype(jnp.bfloat16).astype(jnp.float32) for d in range(3)
    ]
    own_i = lab_ref[x + 1]
    line = lax.broadcasted_iota(jnp.int32, (CY, CZ), 0)
    deep = lax.broadcasted_iota(jnp.int32, (CY, CZ), 1)
    edge_line = own_i if line_ref is None else jnp.broadcast_to(line_ref[pl.ds(x, 1), :], (CY, CZ))
    own = own_i.astype(jnp.float32)
    oth_x = lab_ref[x].astype(jnp.float32)
    oth_y = jnp.where(line > 0, pltpu.roll(own_i, 1, 0), edge_line).astype(jnp.float32)
    oth_z = jnp.where(deep > 0, pltpu.roll(own_i, 1, 1), -1).astype(jnp.float32)
    same_xy = oth_x == oth_y
    same_xz = oth_x == oth_z
    same_yz = oth_y == oth_z
    sum_x = affin[0] + jnp.where(same_xy, affin[1], 0.0) + jnp.where(same_xz, affin[2], 0.0)
    sum_y = affin[1] + jnp.where(same_yz, affin[2], 0.0)
    top_x = sum_x.astype(jnp.bfloat16).astype(jnp.float32)
    top_y = sum_y.astype(jnp.bfloat16).astype(jnp.float32)
    in_x = same_xy | same_xz
    rest = jnp.where(in_x, sum_x - top_x, sum_y - top_y)
    rest_at = jnp.where(in_x, oth_x, oth_y)

    ids = lax.broadcasted_iota(jnp.int32, (LABELS, CZ), 0).astype(jnp.float32).astype(jnp.bfloat16)

    def spread_row(values, y):
        wide = jnp.broadcast_to(values[y : y + 1, :], (16, CZ)).astype(jnp.bfloat16)
        return jnp.concatenate([wide] * (LABELS // 16), axis=0)

    zero = jnp.zeros((LABELS, CZ), jnp.bfloat16)
    one = jnp.ones((LABELS, CZ), jnp.bfloat16)
    lefts, tops, rests = [], [], []
    for y in rows:
        lefts.append(jnp.where(spread_row(own, y) == ids, one, zero))
        tops.append(
            jnp.where(
                spread_row(oth_x, y) == ids,
                spread_row(top_x, y),
                jnp.where(
                    spread_row(oth_y, y) == ids,
                    spread_row(top_y, y),
                    jnp.where(spread_row(oth_z, y) == ids, spread_row(affin[2], y), zero),
                ),
            )
        )
        rests.append(jnp.where(spread_row(rest_at, y) == ids, spread_row(rest, y), zero))
    left = jnp.concatenate(lefts, axis=1)
    right = jnp.concatenate(
        [jnp.concatenate(tops, axis=1), jnp.concatenate(rests, axis=1)], axis=0
    )
    found = lax.dot_general(
        right, left, (((1,), (1,)), ((), ())), preferred_element_type=jnp.float32
    )
    return found[:LABELS] + found[LABELS:]


def two_terms(value, axis):
    top = value.astype(jnp.bfloat16)
    rest = (value - top.astype(jnp.float32)).astype(jnp.bfloat16)
    return jnp.concatenate([top, rest], axis=axis)


def one_hot(mask):
    return jnp.where(mask, 1.0, 0.0).astype(jnp.bfloat16)


def slot_rows(table, ends_ref, owner_ref, row_ref, count_ref):
    first = ends_ref[0, 0:1, :]
    second = ends_ref[0, 1:2, :]
    label = lax.broadcasted_iota(jnp.int32, (LABELS, SLOTS), 0)
    slot = lax.broadcasted_iota(jnp.int32, (1, SLOTS), 1)
    both = table + table.T
    picked = jnp.dot(
        two_terms(both, 0), one_hot(first == label), preferred_element_type=jnp.float32
    )
    picked = picked[:LABELS] + picked[LABELS:]
    value = jnp.sum(jnp.where(second == label, picked, 0.0), axis=0, keepdims=True)
    keep = (slot < count_ref[...]) & (first != second)
    value = jnp.where(keep, value, 0.0)
    row_id = lax.broadcasted_iota(jnp.int32, (EO, SLOTS), 0)
    spread = lax.dot_general(
        two_terms(jnp.where(owner_ref[...] == row_id, value, 0.0), 0),
        one_hot(row_ref[...] == row_id),
        (((1,), (1,)), ((), ())),
        preferred_element_type=jnp.float32,
    )
    return spread[:EO] + spread[EO:]


def whole_kernel(
    f_ref,
    own_hbm,
    conv_hbm,
    row_bias_hbm,
    head_hbm,
    head_bias_hbm,
    ends_hbm,
    owner_hbm,
    row_hbm,
    count_hbm,
    o_ref,
    conv_ref,
    row_bias_ref,
    head_ref,
    head_bias_ref,
    ends_ref,
    owner_ref,
    row_ref,
    count_ref,
    bias_ref,
    fbuf_ref,
    p_ref,
    lab_ref,
    line_ref,
    last_line_ref,
    w_ref,
    logit_a,
    logit_b,
    sums_a,
    sums_b,
    table_ref,
    rows_ref,
    got_ref,
    small_sem,
    load_sem,
    y_send,
    y_recv,
    x_send,
    x_recv,
    row_send,
    row_recv,
):
    bx = lax.axis_index("bx")
    by = lax.axis_index("by")
    xm = lax.rem(bx + NBX - 1, NBX)
    xp = lax.rem(bx + 1, NBX)
    ym = lax.rem(by + NBY - 1, NBY)
    yp = lax.rem(by + 1, NBY)
    me = bx * NBY + by
    barrier = pltpu.get_barrier_semaphore()

    lines = [lax.rem(by + step, NBY) for step in range(NBY)]

    def all_peers(visit):
        def one_x(step, carry):
            peer_x = lax.rem(bx + step, NBX)
            for n in range(NBY):
                visit(peer_x, lines[n], step * NBY + n)
            return carry

        for n in range(1, NBY):
            visit(bx, lines[n], n)
        lax.fori_loop(1, NBX, one_x, 0)

    def greet(peer_x, peer_y, slot):
        pl.semaphore_signal(barrier, inc=1, device_id=(peer_x, peer_y), device_id_type=MESH)

    def load(pair):
        at = pl.ds(2 * pair, 2)
        return pltpu.make_async_copy(f_ref.at[:, at], fbuf_ref.at[:, at], load_sem.at[pair])

    small = [
        pltpu.make_async_copy(src, dst, small_sem.at[n])
        for n, (src, dst) in enumerate(
            [
                (conv_hbm, conv_ref),
                (own_hbm, lab_ref.at[pl.ds(1, CX)]),
                (row_bias_hbm, row_bias_ref),
                (head_hbm, head_ref),
                (head_bias_hbm, head_bias_ref),
                (ends_hbm, ends_ref),
                (owner_hbm, owner_ref),
                (row_hbm, row_ref),
                (count_hbm, count_ref),
            ]
        )
    ]
    for copy in small:
        copy.start()
    for pair in (7, 0, 1, 2, 3, 4, 5, 6):
        load(pair).start()

    all_peers(greet)
    for copy in small:
        copy.wait()
    last_line_ref[...] = lab_ref[1:, CY - 1, :]
    diagonal = lax.broadcasted_iota(jnp.int32, (C, C), 0) == lax.broadcasted_iota(
        jnp.int32, (C, C), 1
    )
    column = jnp.sum(jnp.where(diagonal, row_bias_ref[...], 0.0), axis=1, keepdims=True)
    for out_y in range(2):
        bias_ref[out_y * C : (out_y + 1) * C, :] = jnp.broadcast_to(column, (C, CZ))
    lay_weights(conv_ref, w_ref)
    to = lax.broadcasted_iota(jnp.int32, (256, 256), 0)
    come = lax.broadcasted_iota(jnp.int32, (256, 256), 1)
    perm = ((to & 15) * 16 + (to >> 4) == come).astype(jnp.float32).astype(jnp.bfloat16)

    def remote(src, dst, send_sem, recv_sem, peer):
        return pltpu.make_async_remote_copy(
            src_ref=src,
            dst_ref=dst,
            send_sem=send_sem,
            recv_sem=recv_sem,
            device_id=peer,
            device_id_type=MESH,
        )

    def y_copies(pair):
        at = pl.ds(1 + 2 * pair, 2)
        return (
            remote(
                p_ref.at[at, 1], p_ref.at[at, CY + 1], y_send.at[0, pair], y_recv.at[0, pair], (bx, ym)
            ),
            remote(
                p_ref.at[at, CY], p_ref.at[at, 0], y_send.at[1, pair], y_recv.at[1, pair], (bx, yp)
            ),
        )

    inner = pl.ds(1, CY)
    x_copies = [
        remote(src, dst, x_send.at[n], x_recv.at[n], peer)
        for n, (src, dst, peer) in enumerate(
            [
                (p_ref.at[1, inner], p_ref.at[CX + 1, inner], (xm, by)),
                (p_ref.at[1, 1], p_ref.at[CX + 1, CY + 1], (xm, ym)),
                (p_ref.at[1, CY], p_ref.at[CX + 1, 0], (xm, yp)),
                (p_ref.at[CX, inner], p_ref.at[0, inner], (xp, by)),
                (p_ref.at[CX, 1], p_ref.at[0, CY + 1], (xp, ym)),
                (p_ref.at[CX, CY], p_ref.at[0, 0], (xp, yp)),
                (lab_ref.at[CX], lab_ref.at[0], (xp, by)),
                (last_line_ref, line_ref, (bx, yp)),
            ]
        )
    ]

    def turn(pair):
        for group in range(C // 16):
            block = jnp.concatenate(
                [
                    fbuf_ref[16 * group : 16 * group + 16, 2 * pair + half].reshape(256, CZ)
                    for half in range(2)
                ],
                axis=1,
            )
            out = jnp.dot(perm, block, preferred_element_type=jnp.float32).astype(jnp.bfloat16)
            for half in range(2):
                p_ref[1 + 2 * pair + half, 1 : CY + 1, 16 * group : 16 * group + 16, :] = out[
                    :, half * CZ : (half + 1) * CZ
                ].reshape(CY, 16, CZ)

    def turned(n, carry):
        pair = lax.rem(n + CX // 2 - 1, CX // 2)
        load(pair).wait()
        turn(pair)
        return carry

    lax.fori_loop(0, 3, turned, 0)
    pl.semaphore_wait(barrier, DEVICES - 1)
    for pair in (CX // 2 - 1, 0, 1):
        for copy in y_copies(pair):
            copy.start()
    for copy in x_copies:
        copy.start()

    def convolve(jobs, logit_ref):
        for pairs, sums_ref in zip(jobs, (sums_a, sums_b)):
            conv_dot(pairs, p_ref, w_ref, sums_ref)
        for pairs, sums_ref in zip(jobs, (sums_a, sums_b)):
            conv_head(pairs, sums_ref, bias_ref, head_ref, head_bias_ref, logit_ref)

    def inner_pairs(at):
        return [(1 + at + m, at + m, j) for m in range(2) for j in range(1, PAIRS - 1)]

    def early(n, carry):
        load(n + 2).wait()
        conv_dot(inner_pairs(2 * n), p_ref, w_ref, sums_a)
        turn(n + 2)
        conv_head(inner_pairs(2 * n), sums_a, bias_ref, head_ref, head_bias_ref, logit_a)
        for copy in y_copies(n + 2):
            copy.start()
        return carry

    lax.fori_loop(0, CX // 2 - 3, early, 0)
    jobs = (inner_pairs(EARLY - 4), inner_pairs(EARLY - 2))
    for pairs, sums_ref in zip(jobs, (sums_a, sums_b)):
        conv_dot(pairs, p_ref, w_ref, sums_ref)
    found = []
    for at, pairs, sums_ref in zip(range(2), jobs, (sums_a, sums_b)):
        found.append(pair_sums(at + 1, at, logit_a, lab_ref, None, INNER_ROWS))
        conv_head(pairs, sums_ref, bias_ref, head_ref, head_bias_ref, logit_a)
    table_ref[...] = found[0] + found[1]

    def inner_sums(n, carry):
        found = [
            pair_sums(at + 1, at, logit_a, lab_ref, None, INNER_ROWS) for at in (2 * n, 2 * n + 1)
        ]
        table_ref[...] += found[0] + found[1]
        return carry

    lax.fori_loop(1, INNER // 2, inner_sums, 0)
    for copy in x_copies:
        copy.wait()
    for pair in range(CX // 2):
        for copy in y_copies(pair):
            copy.wait()

    @pl.when(bx == 0)
    def _():
        p_ref[0] = jnp.zeros((CY + 2, C, CZ), jnp.bfloat16)
        lab_ref[0] = jnp.full((CY, CZ), -1, jnp.int32)

    @pl.when(bx == NBX - 1)
    def _():
        p_ref[CX + 1] = jnp.zeros((CY + 2, C, CZ), jnp.bfloat16)

    @pl.when(by == 0)
    def _():
        p_ref[:, 0] = jnp.zeros((CX + 2, C, CZ), jnp.bfloat16)
        line_ref[...] = jnp.full((CX, CZ), -1, jnp.int32)

    @pl.when(by == NBY - 1)
    def _():
        p_ref[:, CY + 1] = jnp.zeros((CX + 2, C, CZ), jnp.bfloat16)

    half = EARLY // 2

    def border(job, carry):
        at = half * job
        pairs = [(1 + at + m, at + m, j) for m in range(half) for j in (0, PAIRS - 1)]
        conv_dot(pairs, p_ref, w_ref, sums_a)
        conv_head(pairs, sums_a, bias_ref, head_ref, head_bias_ref, logit_a)
        return carry

    lax.fori_loop(0, 2, border, 0)

    ends = (CX - 1, 0)
    jobs = [[(x, k, j) for j in range(PAIRS)] for k, x in enumerate(ends)]
    for pairs, sums_ref in zip(jobs, (sums_a, sums_b)):
        conv_dot(pairs, p_ref, w_ref, sums_ref)
    found = []
    for at, pairs, sums_ref in zip((INNER, INNER + 1), jobs, (sums_a, sums_b)):
        found.append(pair_sums(at + 1, at, logit_a, lab_ref, line_ref))
        conv_head(pairs, sums_ref, bias_ref, head_ref, head_bias_ref, logit_b)
    table_ref[...] += found[0] + found[1]

    def late(n, carry):
        found = [pair_sums(k + 1, k, logit_a, lab_ref, line_ref) for k in (2 * n, 2 * n + 1)]
        table_ref[...] += found[0] + found[1]
        return carry

    lax.fori_loop(INNER // 2 + 1, EARLY // 2, late, 0)
    found = [pair_sums(x, k, logit_b, lab_ref, line_ref) for k, x in enumerate(ends)]
    found += [pair_sums(at + 1, at, logit_a, lab_ref, line_ref, BORDER_ROWS) for at in range(INNER)]
    table_ref[...] += functools.reduce(jnp.add, found)
    rows = slot_rows(table_ref[...], ends_ref, owner_ref, row_ref, count_ref)
    for n in range(EO):
        rows_ref[n] = rows[n : n + 1, :]

    def give(peer_x, peer_y, slot):
        mine = rows_ref.at[peer_x * NBY + peer_y]
        remote(mine, got_ref.at[slot], row_send, row_recv, (peer_x, peer_y)).start()

    all_peers(give)
    others = pl.ds(1, DEVICES - 1)
    remote(
        rows_ref.at[others], got_ref.at[others], row_send, row_recv, (bx, lines[1])
    ).wait()
    totals = [rows_ref[me], got_ref[1], got_ref[2], got_ref[3]]
    for step in range(4, DEVICES):
        totals[step % 4] = totals[step % 4] + got_ref[step]
    total = (totals[0] + totals[1]) + (totals[2] + totals[3])
    o_ref[...] = total


def on_device(
    features,
    labels,
    conv_weight,
    conv_bias,
    head_weight,
    head_bias,
    edge_ends,
    edge_owner,
    edge_row,
    edge_count,
):
    bf16, f32, i32 = jnp.bfloat16, jnp.float32, jnp.int32
    total = pl.pallas_call(
        whole_kernel,
        out_shape=jax.ShapeDtypeStruct((1, EO), f32),
        in_specs=[pl.BlockSpec(memory_space=pl.ANY)] * 10,
        out_specs=VMEM,
        scratch_shapes=[
            pltpu.VMEM((C, 27 * C), bf16),
            pltpu.VMEM((1, C), f32),
            pltpu.VMEM((3, C), bf16),
            pltpu.SMEM((3,), f32),
            pltpu.VMEM((1, 2, SLOTS), i32),
            pltpu.VMEM((1, SLOTS), i32),
            pltpu.VMEM((1, SLOTS), i32),
            pltpu.VMEM((1, 1), i32),
            pltpu.VMEM((2 * C, CZ), f32),
            pltpu.VMEM((C, CX, CY, CZ), bf16),
            pltpu.VMEM((CX + 2, CY + 2, C, CZ), bf16),
            pltpu.VMEM((CX + 1, CY, CZ), i32),
            pltpu.VMEM((CX, CZ), i32),
            pltpu.VMEM((CX, CZ), i32),
            pltpu.VMEM((6 * C, 12 * C), bf16),
            pltpu.VMEM((EARLY, 3, CY, CZ), f32),
            pltpu.VMEM((CX - EARLY, 3, CY, CZ), f32),
            pltpu.VMEM((6 * C, EARLY * CZ), f32),
            pltpu.VMEM((6 * C, EARLY * CZ), f32),
            pltpu.VMEM((LABELS, LABELS), f32),
            pltpu.VMEM((DEVICES, 1, EO), f32),
            pltpu.VMEM((DEVICES, 1, EO), f32),
            pltpu.SemaphoreType.DMA((9,)),
            pltpu.SemaphoreType.DMA((CX // 2,)),
            pltpu.SemaphoreType.DMA((2, CX // 2)),
            pltpu.SemaphoreType.DMA((2, CX // 2)),
            pltpu.SemaphoreType.DMA((8,)),
            pltpu.SemaphoreType.DMA((8,)),
            pltpu.SemaphoreType.DMA,
            pltpu.SemaphoreType.DMA,
        ],
        compiler_params=pltpu.CompilerParams(
            collective_id=0, has_side_effects=True, vmem_limit_bytes=63 * 2**20
        ),
        name="whole",
    )(
        features,
        labels,
        conv_weight,
        conv_bias[None],
        head_weight,
        head_bias,
        edge_ends,
        edge_owner[:, :, 0],
        edge_row,
        edge_count[None],
    )
    return total[0]


def solution(mesh):
    placed = (
        P(None, "bx", "by", None),
        P("bx", "by", None),
        P(),
        P(),
        P(),
        P(),
        P(("bx", "by"), None, None),
        P(("bx", "by"), None, None),
        P(("bx", "by"), None),
        P(("bx", "by")),
    )
    return jax.shard_map(
        on_device, mesh=mesh, in_specs=placed, out_specs=P(("bx", "by")), check_vma=False
    )
```
